128 devices in a mesh: slab: 16 (over x, y), span: 8 (over z, core).
Axes of the slice: x: 4, y: 4, z: 4, core: 2. Of those that a mesh axis runs over, the one named last changes fastest.
Arguments:
- velocity: float32 [3, 128, 256, 512], P(None, 'slab', 'span'), may hold values from -6 to 6
- profile: float32 [32, 3, 262144], P(None, None, ('slab', 'span')), may hold values from -3 to 3
- normal: float32 [3, 262144], P(None, ('slab', 'span')), may hold values from -1 to 1, as said below
- height: float32 [262144], P(('slab', 'span')), may hold values from 0.5 to 2
- pressure_grad: float32 [3, 262144], P(None, ('slab', 'span')), may hold values from -8 to 8
- owner_device: int32 [262144, 1], P(('slab', 'span')), may hold values from 0 to 127; in each aligned block of 2048 rows (0 to 2047, 2048 to 4095, ...) at most 32 rows name the same one
- match_cell: int32 [262144], P(('slab', 'span')), may hold values from 0 to 131071
Outputs:
- new_velocity: float32 [3, 128, 256, 512], P(None, 'slab', 'span')
- wall_profile: float32 [32, 3, 262144], P(None, None, ('slab', 'span'))
- wall_stress: float32 [3, 262144], P(None, ('slab', 'span'))
The draws below stay inside these ranges and needn't reach their ends.
Inputs may be any that keep to these rules, and one draw needn't show every extreme that they name: `owner_device`: among the 2048 hull cells of one device (aligned blocks of rows), at most 32 have their matching cell on any one device, and exactly 32 on some device. `match_cell`: A local index (x * 32 + y) * 512 + z within the owner's block of the volume. `normal`: each column is a unit vector with vertical component between -0.9 and 0.9.
All inputs are finite; a program needn't handle non-finite values.
Results may differ from the reference program's by a relative error of at most 0.0003.
Values sent between devices are 32-bit elements; how exact they have to be, the bound alone decides.
A program may use at most 192 MiB of HBM per device.

```python
import math
import jax
import jax.numpy as jnp
import numpy as np
from jax import lax

CX = 8
CY = 32
NZ = 512
NW = 32
PICARD = 2
HULL_DEV = 2048
MOST = 32
NX = 128
NY = 256
HULL = 262144
N_SPAN = 8
DEVICES = 128


def draw_normal(key, part):
    key_a, key_b = jax.random.split(key)
    azimuth = jax.random.uniform(key_a, (HULL,), jnp.float32, -math.pi, math.pi)
    vertical = jax.random.uniform(key_b, (HULL,), jnp.float32, -0.9, 0.9)
    radial = jnp.sqrt(1.0 - vertical * vertical)
    return jnp.stack([radial * jnp.cos(azimuth), radial * jnp.sin(azimuth), vertical])


def touch_ends(values, rng, low, high):
    place = [jax.random.randint(jax.random.fold_in(rng, axis), (), 0, length) for axis, length in enumerate(values.shape)]
    main_axis = values.shape.index(max(values.shape))
    neighbour = place[:main_axis] + [(place[main_axis] + 1) % values.shape[main_axis]] + place[main_axis + 1:]
    return values.at[tuple(place)].set(low).at[tuple(neighbour)].set(high)


def level_of(key, shape, cuts, smallest, high):
    def one(position, parts):
        steps = jax.random.uniform(jax.random.fold_in(jax.random.fold_in(key, 6), position), (parts,), jnp.float32, smallest / len(cuts), high / len(cuts))
        return jnp.repeat(jnp.exp(steps), shape[position] // parts).reshape((-1,) + (1,) * (len(shape) - position - 1))

    gain = one(*cuts[0])
    for cut in cuts[1:]:
        gain = gain * one(*cut)
    return gain


def routed_block(stream_key, own, number, rows, number_of, top, limit, lean):
    order = jax.random.permutation(stream_key, number_of)
    heavy_load, ordinary = portions_of(number_of, rows * top, limit, lean, True), portions_of(number_of, rows * top, limit, lean, False)
    places = jnp.arange(number_of)

    def named(tallies, offset_by):
        used = int((tallies > 0).sum())
        fixed = max(1, used // 4)
        shifted = fixed + (places - fixed + offset_by * (used - fixed)) % max(1, number_of - fixed)
        return jnp.zeros((number_of,), jnp.int32).at[order[jnp.where(places < fixed, places, shifted)]].set(jnp.asarray(tallies, jnp.int32))

    tallies = jnp.where(number % 4 == 0, named(heavy_load, number // 4), named(ordinary, number - number // 4 - 1))
    mixed = jax.random.permutation(jax.random.fold_in(own, 3), number_of)
    giver, taker = mixed[0:number_of // 2 * 2:2], mixed[1:number_of // 2 * 2:2]
    margin = jnp.minimum(tallies[giver] - 1, limit - tallies[taker]) // 2
    margin = jnp.where((giver == order[0]) | (taker == order[0]) | (tallies[taker] == 0), 0, jnp.maximum(margin, 0))
    shifted = jax.random.randint(jax.random.fold_in(own, 4), (number_of // 2,), 0, 1 << 20) % (margin + 1)
    tallies = tallies.at[giver].add(-shifted).at[taker].add(shifted)
    labels = jnp.searchsorted(jnp.cumsum(tallies), jnp.arange(rows * top), side="right").astype(jnp.int32)
    table = labels.reshape(top, rows).T
    table = table[jax.random.permutation(jax.random.fold_in(own, 1), rows)]
    offset_by = jax.random.randint(jax.random.fold_in(own, 2), (rows, 1), 0, top)
    return jnp.take_along_axis(table, (jnp.arange(top)[None, :] + offset_by) % top, axis=1)


def portions_of(amount, total, limit, skew, full):
    portions = [(1 << 20) // math.isqrt(rank ** skew) + 1 for rank in range(1, amount + 1)]
    largest = limit if full else min(limit, max(-(-total // amount), total * portions[0] // sum(portions)))
    least = 1 if total - largest >= amount - 1 else 0
    given, surplus = [largest] + [least] * (amount - 1), total - largest - least * (amount - 1)
    while surplus > 0:
        movable = [i for i in range(1, amount) if given[i] < largest] or [i for i in range(1, amount) if given[i] < limit]
        mass, budget = sum([portions[i] for i in movable]), surplus
        for i in movable:
            more = min(limit - given[i], max(1, budget * portions[i] // mass), surplus)
            given[i] = given[i] + more
            surplus = surplus - more
    return np.array(given)


def noise(key, shape, width, limit, shards=(), held_as=jnp.bfloat16):
    loudness = level_of(key, shape, shards, -0.22, 0.18) if shards else 1.0
    result = jax.random.normal(key, shape, jnp.float32) * width * loudness
    return jnp.minimum(jnp.maximum(result, -limit), limit).astype(held_as)


def setup_inputs(seed: int = 0) -> dict:
    arg_keys = jax.random.split(jax.random.key(seed), 8)
    velocity = noise(arg_keys[0], (3, NX, NY, NZ), 1.0, 6.0, ((1, 16), (2, 8)), jnp.float32)
    profile = noise(arg_keys[1], (NW, 3, HULL), 0.5, 3.0, ((2, 128),), jnp.float32)
    normal = draw_normal(jax.random.fold_in(arg_keys[7], 71), 0)
    height = jnp.clip(jnp.exp(math.log(2.0) - 1.3862944 * jax.random.uniform(arg_keys[3], (HULL,), jnp.float32) ** level_of(arg_keys[3], (HULL,), ((0, 128),), -0.2, 0.2)), 0.5, 2.0)
    pressure_grad = noise(arg_keys[4], (3, HULL), 2.0, 8.0, ((1, 128),), jnp.float32)
    owner_device_keys = jax.random.split(jax.random.fold_in(arg_keys[5], 1), HULL // HULL_DEV)
    owner_device_turns = jax.random.permutation(jax.random.fold_in(arg_keys[5], 3), HULL // HULL_DEV)
    owner_device = jax.vmap(lambda own, number: routed_block(jax.random.fold_in(arg_keys[5], 2), own, number, HULL_DEV, DEVICES, 1, MOST, 1))(owner_device_keys, owner_device_turns).reshape((HULL, 1))
    match_cell = touch_ends(jax.random.randint(arg_keys[6], (HULL,), 0, CX * CY * NZ), jax.random.fold_in(arg_keys[6], 1), 0, (CX * CY * NZ) - 1).astype(jnp.int32)
    return dict(velocity=velocity, profile=profile, normal=normal, height=height, pressure_grad=pressure_grad, owner_device=owner_device, match_cell=match_cell)


time_step = 0.1
viscosity = 0.001
smag_coef = 0.02
kappa_coef = 0.41
damping_plus = 26.0
stretch = 1.12
area_ratio = 4.0
third_part = 1.0 / 3.0
two_thirds = 2.0 / 3.0

def rhs_core(padded):
    extended = jnp.pad(padded, ((0, 0), (0, 0), (0, 0), (1, 1)))
    center = extended[:, 1:-1, 1:-1, 1:-1]
    x_plus = extended[:, 2:, 1:-1, 1:-1]
    x_minus = extended[:, :-2, 1:-1, 1:-1]
    y_plus = extended[:, 1:-1, 2:, 1:-1]
    y_minus = extended[:, 1:-1, :-2, 1:-1]
    z_plus = extended[:, 1:-1, 1:-1, 2:]
    z_minus = extended[:, 1:-1, 1:-1, :-2]
    grad_x = 0.5 * (x_plus - x_minus)
    grad_y = 0.5 * (y_plus - y_minus)
    grad_z = 0.5 * (z_plus - z_minus)
    laplace = x_plus + x_minus + y_plus + y_minus + z_plus + z_minus - 6.0 * center
    shear = jnp.sqrt(lax.optimization_barrier(jnp.sum(grad_x * grad_x + grad_y * grad_y + grad_z * grad_z, axis=0)))
    eddy_visc = viscosity + smag_coef * shear
    advect = center[0:1] * grad_x + center[1:2] * grad_y + center[2:3] * grad_z
    return eddy_visc[None] * laplace - advect

def pad_plane(field):
    return jnp.pad(field, ((0, 0), (1, 1), (1, 1), (0, 0)))

def thomas(sub_diag, main_diag, super_diag, right_side):

    def forward(carry, element):
        prev_c, prev_d = carry
        low_coef, mid_coef, up_coef, source = element
        divisor = mid_coef - low_coef * prev_c
        next_c = up_coef / divisor
        next_d = (source - low_coef[None] * prev_d) / divisor[None]
        return ((next_c, next_d), (next_c, next_d))
    start_carry = (jnp.zeros_like(main_diag[0]), jnp.zeros_like(right_side[0]))
    _, (reduced_c, reduced_d) = lax.scan(forward, start_carry, (sub_diag, main_diag, super_diag, right_side))

    def backward(following, element):
        up_coef, source = element
        solved = source - up_coef[None] * following
        return (solved, solved)
    _, values = lax.scan(backward, jnp.zeros_like(right_side[0]), (reduced_c, reduced_d), reverse=True)
    return values

def tangential(vector, normal):
    return vector - lax.optimization_barrier(jnp.sum(vector * normal, axis=0, keepdims=True)) * normal

def wall_model(profile, matched, normal, height, pressure_grad):
    points = profile.shape[0]
    levels = jnp.arange(points + 2, dtype=jnp.float32)
    fraction = (stretch ** levels - 1.0) / (stretch ** (points + 1) - 1.0)
    heights = fraction[:, None] * height[None, :]
    target = tangential(matched, normal)
    forcing = tangential(pressure_grad, normal)
    spacing = heights[1:] - heights[:-1]
    face_height = 0.5 * (heights[1:] + heights[:-1])
    cell_span = 0.5 * (heights[2:] - heights[:-2])
    first_height = heights[1]
    current = profile
    for sweep in range(PICARD):
        stress = viscosity * current[0] / first_height[None]
        speed = jnp.sqrt(jnp.sqrt(lax.optimization_barrier(jnp.sum(stress * stress, axis=0))))
        damping = 1.0 - jnp.exp(-face_height * speed[None] / (viscosity * damping_plus))
        diffusivity = viscosity + kappa_coef * face_height * speed[None] * damping * damping
        conductance = diffusivity / spacing
        lower_w = conductance[:-1] / cell_span
        upper_w = conductance[1:] / cell_span
        sub_diag = -time_step * lower_w
        super_diag = -time_step * upper_w
        main_diag = 1.0 + time_step * (lower_w + upper_w)
        right_side = profile - time_step * forcing[None]
        right_side = right_side.at[-1].add(time_step * upper_w[-1][None] * target)
        current = thomas(sub_diag, main_diag, super_diag, right_side)
    stress = viscosity * current[0] / first_height[None]
    return (current, stress)

def reference(velocity, profile, normal, height, pressure_grad, owner_device, match_cell):
    section_one = velocity + time_step * rhs_core(pad_plane(velocity))
    section_two = 0.75 * velocity + 0.25 * (section_one + time_step * rhs_core(pad_plane(section_one)))
    section_three = third_part * velocity + two_thirds * (section_two + time_step * rhs_core(pad_plane(section_two)))
    device_of = owner_device[:, 0].astype(jnp.int32)
    slab_of = device_of // N_SPAN
    span_of = device_of % N_SPAN
    plane_of = match_cell // (CY * NZ)
    row_of = match_cell // NZ % CY
    depth_of = (match_cell % NZ).astype(jnp.int32)
    global_x = (slab_of * CX + plane_of).astype(jnp.int32)
    global_y = (span_of * CY + row_of).astype(jnp.int32)
    matched = velocity[:, global_x, global_y, depth_of]
    wall_profile, wall_stress = wall_model(profile, matched, normal, height, pressure_grad)
    push = -time_step * area_ratio * wall_stress
    new_velocity = section_three.at[:, global_x, global_y, depth_of].add(push)
    return (new_velocity, wall_profile, wall_stress)
```

```python
import jax
import jax.numpy as jnp
import numpy as np
from jax import lax
from jax.experimental import pallas as pl
from jax.experimental.pallas import tpu as pltpu
from jax.sharding import PartitionSpec as P

MESH = pl.DeviceIdType.MESH
BF16, F32, I32 = jnp.bfloat16, jnp.float32, jnp.int32

DEVICES = 128
SLOTS = 32
TILE = 128
TILES = 16
LEVELS = 32
CX, CY, ZB = 8, 32, 4
XY = CX * CY
NZ = 512
TOP = 8
MIB = 1 << 20

time_step = 0.1
viscosity = 0.001
smag_coef = 0.02
kappa_coef = 0.41
damping_plus = 26.0
stretch = 1.12
area_ratio = 4.0

FRAC = (stretch ** np.arange(LEVELS + 2) - 1.0) / (stretch ** (LEVELS + 1) - 1.0)
SPACING = FRAC[1:] - FRAC[:-1]
FACE = 0.5 * (FRAC[1:] + FRAC[:-1])
SPAN = 0.5 * (FRAC[2:] - FRAC[:-2])
LOWER = [float(v) for v in time_step / (SPACING[:-1] * SPAN)]
UPPER = [float(v) for v in time_step / (SPACING[1:] * SPAN)]


def dot_nn(a, b):
    return lax.dot_general(a, b, (((1,), (0,)), ((), ())), preferred_element_type=F32)


def dot_nt(a, b):
    return lax.dot_general(a, b, (((1,), (1,)), ((), ())), preferred_element_type=F32)


def split(value):
    high = value.astype(BF16)
    return high, (value - high.astype(F32)).astype(BF16)


def columns(j):
    return pl.ds(j * TILE, TILE)


def build_request(owner, cell, onehot, rank, picked, message):
    rows = lax.broadcasted_iota(I32, (TILE, TILE), 0)
    lanes = lax.broadcasted_iota(I32, (TILE, TILE), 1)
    earlier = jnp.where(rows < lanes, 1.0, 0.0).astype(BF16)
    summing = jnp.concatenate([earlier, jnp.ones((TILE, TILE), BF16)], axis=1)
    slots = lax.broadcasted_iota(I32, (SLOTS, TILE), 0)
    taken = jnp.zeros((TILE, TILE), F32)
    for j in range(TILES):
        mine = rows == owner[j : j + 1, :]
        one = jnp.where(mine, 1.0, 0.0).astype(BF16)
        onehot[:, columns(j)] = one
        counts = dot_nn(one, summing)
        place = jnp.sum(jnp.where(mine, counts[:, :TILE] + taken, 0.0), axis=0, keepdims=True).astype(I32)
        taken = taken + counts[:, TILE:]
        rank[j : j + 1, :] = place
        at = cell[j : j + 1, :]
        slot = slots == place
        depth = at & (NZ - 1)
        for part, value in enumerate((at >> 9, depth & (NZ - 2), depth & 1)):
            picked[part * SLOTS : (part + 1) * SLOTS, columns(j)] = jnp.where(slot, value.astype(F32), 0.0).astype(BF16)
    message[:, 0, :] = dot_nt(onehot[...], picked[...])


def read_request(arrived, request):
    turned = arrived[:, 0, :].T
    request[0:SLOTS, :] = turned[0:SLOTS].astype(I32)
    request[SLOTS : 2 * SLOTS, :] = (turned[SLOTS : 2 * SLOTS] + turned[2 * SLOTS : 3 * SLOTS]).astype(I32)


def gather_cells(request, depth_hot, v_high, v_low, gathered, message):
    depths = lax.broadcasted_iota(I32, (NZ, TILE), 0)
    planes = lax.broadcasted_iota(I32, (XY, TILE), 0)

    @pl.loop(0, SLOTS // 2)
    def _(pair):
        for half in range(2):
            slot = pair * 2 + half
            row = request[pl.ds(SLOTS + slot, 1), :]
            depth_hot[pair, :, columns(half)] = jnp.where(depths == row, 1.0, 0.0).astype(BF16)
        hot = depth_hot[pair]
        for c in range(3):
            part = pl.ds(c * XY, XY)
            found = dot_nn(v_high[part, :], hot) + dot_nn(v_low[part, :], hot)
            for half in range(2):
                slot = pair * 2 + half
                where = planes == request[pl.ds(slot, 1), :]
                gathered[pl.ds(c * SLOTS + slot, 1), :] = jnp.sum(
                    jnp.where(where, found[:, half * TILE : (half + 1) * TILE], 0.0), axis=0, keepdims=True
                )

    message[:, 0, :] = gathered[...].T


def scatter_cells(request, depth_hot, arrived, pushes, a_high, a_low, base, out):
    planes = lax.broadcasted_iota(I32, (XY, TILE), 0)
    pushes[...] = arrived[:, 0, :].T

    @pl.loop(0, 3)
    def _(c):
        for slot in range(SLOTS):
            where = planes == request[slot : slot + 1, :]
            push = pushes[pl.ds(c * SLOTS + slot, 1), :]
            high = push.astype(BF16).astype(F32)
            low = push - high
            a_high[slot // 2, :, columns(slot % 2)] = jnp.where(where, high, 0.0).astype(BF16)
            a_low[slot // 2, :, columns(slot % 2)] = jnp.where(where, low, 0.0).astype(BF16)
        for side in range(2):
            total = jnp.zeros((XY, 256), F32)
            for pair in range(SLOTS // 2):
                hot = depth_hot[pair, side * 256 : (side + 1) * 256, :]
                total = total + dot_nt(a_high[pair], hot) + dot_nt(a_low[pair], hot)
            for half in range(2):
                zb = side * 2 + half
                for x in range(CX):
                    block = total[x * CY : (x + 1) * CY, half * TILE : (half + 1) * TILE]
                    out[c, x, zb] = base[c, x, zb] + block


def prepare(field, v_high, v_low):
    @pl.loop(0, 3 * CX)
    def _(i):
        c, x = i // CX, i % CX
        for zb in range(ZB):
            high, low = split(field[c, x + 1, zb, TOP : TOP + CY, :])
            rows = pl.ds(pl.multiple_of(i * CY, CY), CY)
            v_high[rows, columns(zb)] = high
            v_low[rows, columns(zb)] = low


def pack_rows(field, edge):
    for side, row in ((0, TOP), (1, TOP + CY - 1)):
        for c in range(3):
            for x in range(CX):
                edge[side, c * CX + x] = field[c, x + 1, :, row, :]


def unpack_rows(field, edge, span, spans, slab, slabs):
    for side, row in ((0, TOP - 1), (1, TOP + CY)):
        for c in range(3):
            for x in range(CX):
                field[c, x + 1, :, row, :] = edge[side, c * CX + x]
    zero_row = jnp.zeros((CX, ZB, TILE), F32)
    zero_plane = jnp.zeros((ZB, CY, TILE), F32)
    for c in range(3):

        @pl.when(span == 0)
        def _():
            field[c, 1 : CX + 1, :, TOP - 1, :] = zero_row

        @pl.when(span == spans - 1)
        def _():
            field[c, 1 : CX + 1, :, TOP + CY, :] = zero_row

        @pl.when(slab == 0)
        def _():
            field[c, 0, :, TOP : TOP + CY, :] = zero_plane

        @pl.when(slab == slabs - 1)
        def _():
            field[c, CX + 1, :, TOP : TOP + CY, :] = zero_plane


def stage(field, first, out, out_x, out_top, keep, mix):
    lane = lax.broadcasted_iota(I32, (8, TILE), 1)
    at_start, at_end = lane == 0, lane == TILE - 1
    zeros = jnp.zeros((8, TILE), F32)

    @pl.loop(0, CX)
    def _(x):
        for y in range(0, CY, 8):
            here = pl.ds(TOP + y, 8)
            center = [[field[c, x + 1, zb, here, :] for zb in range(ZB)] for c in range(3)]
            ahead = [[pltpu.roll(v, TILE - 1, 1) for v in row] for row in center]
            behind = [[pltpu.roll(v, 1, 1) for v in row] for row in center]
            for zb in range(ZB):
                mid = [center[c][zb] for c in range(3)]
                shear = zeros
                lap, grads = [], []
                for c in range(3):
                    xp, xm = field[c, x + 2, zb, here, :], field[c, x, zb, here, :]
                    yp, ym = field[c, x + 1, zb, pl.ds(TOP + y + 1, 8), :], field[c, x + 1, zb, pl.ds(TOP + y - 1, 8), :]
                    zp = jnp.where(at_end, ahead[c][zb + 1] if zb + 1 < ZB else zeros, ahead[c][zb])
                    zm = jnp.where(at_start, behind[c][zb - 1] if zb else zeros, behind[c][zb])
                    gx, gy, gz = xp - xm, yp - ym, zp - zm
                    shear = shear + (gx * gx + gy * gy + gz * gz)
                    lap.append(((xp + xm) + (yp + ym)) + ((zp + zm) - 6.0 * mid[c]))
                    grads.append(mid[0] * gx + mid[1] * gy + mid[2] * gz)
                eddy = viscosity + (0.5 * smag_coef) * jnp.sqrt(shear)
                for c in range(3):
                    moved = mid[c] + time_step * (eddy * lap[c] - 0.5 * grads[c])
                    if keep:
                        moved = keep * first[c, x + 1, zb, here, :] + mix * moved
                    out[c, x + out_x, zb, pl.ds(out_top + y, 8), :] = moved


def tangential(vector, normal):
    along = vector[0] * normal[0] + vector[1] * normal[1] + vector[2] * normal[2]
    return [vector[c] - along * normal[c] for c in range(3)]


def level(ref, c, k):
    return ref[c, pl.ds(k, TILES, stride=LEVELS), :]


def diffusivity(first, height, inverse2):
    ratio = float((viscosity / FRAC[1]) ** 2)
    square = (first[0] * first[0] + first[1] * first[1] + first[2] * first[2]) * inverse2 * ratio
    scaled = height * jnp.sqrt(jnp.sqrt(square))

    def at(k):
        damping = 1.0 - jnp.exp(scaled * float(-FACE[k] / (viscosity * damping_plus)))
        return viscosity + (float(kappa_coef * FACE[k]) * scaled) * (damping * damping)

    return at


def sweep_one(profile, height, inverse2, forcing, kept):
    at = diffusivity([level(profile, c, 0) for c in range(3)], height, inverse2)
    above = at(LEVELS)
    ratio = jnp.zeros((TILES, TILE), F32)
    value = [jnp.zeros((TILES, TILE), F32)] * 3
    answer = jnp.ones((TILES, TILE), F32)
    for k in range(LEVELS - 1, -1, -1):
        below = at(k)
        low = (below * inverse2) * LOWER[k]
        up = (above * inverse2) * UPPER[k]
        inverse = 1.0 / (1.0 + low + up * (1.0 - ratio))
        ratio = low * inverse
        value = [(level(profile, c, k) - time_step * forcing[c] + up * value[c]) * inverse for c in range(3)]
        answer = answer * (up * inverse)
        above = below
    for c in range(3):
        kept[c] = value[c]
    kept[3] = answer


def sweep_two(profile, height, inverse2, forcing, target, kept, ratios, values):
    at = diffusivity([kept[c] + kept[3] * target[c] for c in range(3)], height, inverse2)
    above = at(LEVELS)
    ratio = jnp.zeros((TILES, TILE), F32)
    value = target
    for k in range(LEVELS - 1, -1, -1):
        below = at(k)
        low = (below * inverse2) * LOWER[k]
        up = (above * inverse2) * UPPER[k]
        inverse = 1.0 / (1.0 + low + up * (1.0 - ratio))
        ratio = low * inverse
        ratios[k] = ratio
        value = [(level(profile, c, k) - time_step * forcing[c] + up * value[c]) * inverse for c in range(3)]
        for c in range(3):
            values[c, k] = value[c]
        above = below
    return value


def substitute(ratios, values, result):
    value = [values[c, 0] for c in range(3)]
    for k in range(LEVELS):
        if k:
            value = [values[c, k] + ratios[k] * value[c] for c in range(3)]
        for c in range(3):
            result[c, pl.ds(k, TILES, stride=LEVELS), :] = value[c]


def take_matched(arrived, onehot, rank, matched):
    high, low = split(arrived[:, 0, :].T)
    slots = lax.broadcasted_iota(I32, (SLOTS, TILE), 0)
    for j in range(TILES):
        one = onehot[:, columns(j)]
        found = dot_nn(high, one) + dot_nn(low, one)
        slot = slots == rank[j : j + 1, :]
        for c in range(3):
            matched[c, j : j + 1, :] = jnp.sum(
                jnp.where(slot, found[c * SLOTS : (c + 1) * SLOTS], 0.0), axis=0, keepdims=True
            )


def send_stress(stress, onehot, rank, picked, picked_low, message):
    slots = lax.broadcasted_iota(I32, (SLOTS, TILE), 0)
    for j in range(TILES):
        slot = slots == rank[j : j + 1, :]
        for c in range(3):
            push = (-time_step * area_ratio) * stress[c, j : j + 1, :]
            high = push.astype(BF16).astype(F32)
            rows = slice(c * SLOTS, (c + 1) * SLOTS)
            picked[rows, columns(j)] = jnp.where(slot, high, 0.0).astype(BF16)
            picked_low[rows, columns(j)] = jnp.where(slot, push - high, 0.0).astype(BF16)
    message[:, 0, :] = dot_nt(onehot[...], picked[...]) + dot_nt(onehot[...], picked_low[...])


def kernel(
    velocity, profile_in, normal_in, height_in, pressure_in, owner, cell,
    new_velocity, wall_profile, wall_stress,
    field_0, field_1, field_2, stepped, v_high, v_low, depth_hot, a_high, a_low,
    onehot, rank, picked, picked_low, request, gathered,
    profile, result, ratios, values, vectors, kept,
    outgoing, incoming, edge_out, edge_in,
    load_sem, profile_sem, store_sem, row_send, row_recv, halo_send, halo_recv,
):
    slab, span = lax.axis_index("slab"), lax.axis_index("span")
    slabs, spans = 16, 8
    me = slab * spans + span
    fields = (field_0, field_1, field_2)

    loads = [
        pltpu.make_async_copy(
            velocity.at[:, :, :, columns(zb)], field_0.at[:, pl.ds(1, CX), zb, pl.ds(TOP, CY), :], load_sem.at[zb]
        )
        for zb in range(ZB)
    ]
    for copy in loads:
        copy.start()
    profile_loads = [
        pltpu.make_async_copy(
            profile_in.at[:, :, columns(j)], profile.at[:, pl.ds(j * LEVELS, LEVELS), :], profile_sem.at[j]
        )
        for j in range(TILES)
    ]
    for copy in profile_loads:
        copy.start()

    barrier = pltpu.get_barrier_semaphore()

    @pl.loop(1, DEVICES)
    def _(i):
        other = lax.rem(me + i, DEVICES)
        pl.semaphore_signal(barrier, 1, device_id=(other // spans, lax.rem(other, spans)), device_id_type=MESH)

    def send_rows(phase):
        @pl.loop(1, DEVICES)
        def _(i):
            other = lax.rem(me + i, DEVICES)
            pltpu.make_async_remote_copy(
                src_ref=outgoing.at[phase, other],
                dst_ref=incoming.at[phase, me],
                send_sem=row_send.at[phase],
                recv_sem=row_recv.at[phase],
                device_id=(other // spans, lax.rem(other, spans)),
                device_id_type=MESH,
            ).start()

        incoming[phase, me] = outgoing[phase, me]

    def await_rows(phase):
        rows = outgoing.at[phase, pl.ds(0, DEVICES - 1)]
        pltpu.make_async_copy(rows, rows, row_send.at[phase]).wait()
        rows = incoming.at[phase, pl.ds(0, DEVICES - 1)]
        pltpu.make_async_copy(rows, rows, row_recv.at[phase]).wait()

    up_x = (lax.rem(slab + 1, slabs), span)
    down_x = (lax.rem(slab + slabs - 1, slabs), span)
    up_y = (slab, lax.rem(span + 1, spans))
    down_y = (slab, lax.rem(span + spans - 1, spans))

    def halo(n):
        field = fields[n]
        inner = pl.ds(TOP, CY)
        ends = (
            (field.at[:, CX, :, inner, :], field.at[:, 0, :, inner, :], up_x),
            (field.at[:, 1, :, inner, :], field.at[:, CX + 1, :, inner, :], down_x),
            (edge_out.at[n, 1], edge_in.at[n, 0], up_y),
            (edge_out.at[n, 0], edge_in.at[n, 1], down_y),
        )
        return [
            pltpu.make_async_remote_copy(
                src_ref=src, dst_ref=dst, send_sem=halo_send.at[n, i], recv_sem=halo_recv.at[n, i],
                device_id=to, device_id_type=MESH,
            )
            for i, (src, dst, to) in enumerate(ends)
        ]

    def send_halo(n):
        pack_rows(fields[n], edge_out.at[n])
        copies = halo(n)
        for copy in copies:
            copy.start()
        return copies

    def await_halo(n, copies):
        for copy in copies:
            copy.wait()
        unpack_rows(fields[n], edge_in.at[n], span, spans, slab, slabs)

    build_request(owner, cell, onehot, rank, picked, outgoing.at[0])
    for copy in loads:
        copy.wait()
    pl.semaphore_wait(barrier, DEVICES - 1)
    send_rows(0)
    copies = send_halo(0)

    for copy in profile_loads:
        copy.wait()
    normal, pressure, matched = vectors.at[0], vectors.at[1], vectors.at[2]
    for c in range(3):
        for j in range(TILES):
            normal[c, j : j + 1, :] = normal_in[c : c + 1, columns(j)]
            pressure[c, j : j + 1, :] = pressure_in[c : c + 1, columns(j)]
    height = height_in[...]
    inverse2 = 1.0 / (height * height)
    forcing = tangential([pressure[c] for c in range(3)], [normal[c] for c in range(3)])
    sweep_one(profile, height, inverse2, forcing, kept)
    prepare(field_0, v_high, v_low)
    await_halo(0, copies)
    stage(field_0, field_0, field_1, 1, TOP, None, None)
    copies = send_halo(1)

    await_rows(0)
    read_request(incoming.at[0], request)
    gather_cells(request, depth_hot, v_high, v_low, gathered, outgoing.at[1])
    send_rows(1)

    await_halo(1, copies)
    stage(field_1, field_0, field_2, 1, TOP, 0.75, 0.25)
    copies = send_halo(2)

    await_rows(1)
    take_matched(incoming.at[1], onehot, rank, matched)
    target = tangential([matched[c] for c in range(3)], [normal[c] for c in range(3)])
    forcing = tangential([pressure[c] for c in range(3)], [normal[c] for c in range(3)])
    first = sweep_two(profile, height, inverse2, forcing, target, kept, ratios, values)
    scale = float(viscosity / FRAC[1]) / height
    stress = vectors.at[3]
    for c in range(3):
        stress[c] = first[c] * scale
    send_stress(stress, onehot, rank, picked, picked_low, outgoing.at[2])
    send_rows(2)

    for c in range(3):
        for j in range(TILES):
            wall_stress[c : c + 1, columns(j)] = stress[c, j : j + 1, :]
    substitute(ratios, values, result)
    profile_stores = [
        pltpu.make_async_copy(
            result.at[:, pl.ds(j * LEVELS, LEVELS), :], wall_profile.at[:, :, columns(j)], profile_sem.at[j]
        )
        for j in range(TILES)
    ]
    for copy in profile_stores:
        copy.start()
    await_halo(2, copies)
    stage(field_2, field_0, stepped, 0, 0, 1.0 / 3.0, 2.0 / 3.0)

    await_rows(2)
    scatter_cells(request, depth_hot, incoming.at[2], gathered, a_high, a_low, stepped, stepped)
    stores = [
        pltpu.make_async_copy(stepped.at[:, :, zb], new_velocity.at[:, :, :, columns(zb)], store_sem.at[zb])
        for zb in range(ZB)
    ]
    for copy in stores:
        copy.start()
    for copy in profile_stores + stores:
        copy.wait()


def per_device(velocity, profile, normal, height, pressure_grad, owner_device, match_cell):
    padded = pltpu.VMEM((3, CX + 2, ZB, CY + 16, TILE), F32)
    hbm, vmem = pl.BlockSpec(memory_space=pl.ANY), pl.BlockSpec(memory_space=pltpu.VMEM)
    new_velocity, wall_profile, wall_stress = pl.pallas_call(
        kernel,
        out_shape=(
            jax.ShapeDtypeStruct(velocity.shape, F32),
            jax.ShapeDtypeStruct((3, LEVELS, TILES * TILE), F32),
            jax.ShapeDtypeStruct((3, TILES * TILE), F32),
        ),
        in_specs=[hbm, hbm, vmem, vmem, vmem, vmem, vmem],
        out_specs=(hbm, hbm, vmem),
        scratch_shapes=[
            padded, padded, padded,
            pltpu.VMEM((3, CX, ZB, CY, TILE), F32),
            pltpu.VMEM((3 * XY, NZ), BF16), pltpu.VMEM((3 * XY, NZ), BF16),
            pltpu.VMEM((SLOTS // 2, NZ, 2 * TILE), BF16),
            pltpu.VMEM((SLOTS // 2, XY, 2 * TILE), BF16), pltpu.VMEM((SLOTS // 2, XY, 2 * TILE), BF16),
            pltpu.VMEM((DEVICES, TILES * TILE), BF16),
            pltpu.VMEM((TILES, TILE), I32),
            pltpu.VMEM((DEVICES, TILES * TILE), BF16), pltpu.VMEM((DEVICES, TILES * TILE), BF16),
            pltpu.VMEM((2 * SLOTS, TILE), I32),
            pltpu.VMEM((DEVICES, TILE), F32),
            pltpu.VMEM((3, TILES * LEVELS, TILE), F32), pltpu.VMEM((3, TILES * LEVELS, TILE), F32),
            pltpu.VMEM((LEVELS, TILES, TILE), F32), pltpu.VMEM((3, LEVELS, TILES, TILE), F32),
            pltpu.VMEM((4, 3, TILES, TILE), F32), pltpu.VMEM((4, TILES, TILE), F32),
            pltpu.VMEM((3, DEVICES, 1, TILE), F32), pltpu.VMEM((3, DEVICES, 1, TILE), F32),
            pltpu.VMEM((3, 2, 3 * CX, ZB, TILE), F32), pltpu.VMEM((3, 2, 3 * CX, ZB, TILE), F32),
            pltpu.SemaphoreType.DMA((ZB,)), pltpu.SemaphoreType.DMA((TILES,)), pltpu.SemaphoreType.DMA((ZB,)),
            pltpu.SemaphoreType.DMA((3,)), pltpu.SemaphoreType.DMA((3,)),
            pltpu.SemaphoreType.DMA((3, 4)), pltpu.SemaphoreType.DMA((3, 4)),
        ],
        compiler_params=pltpu.CompilerParams(
            collective_id=0, has_side_effects=True, vmem_limit_bytes=52 * MIB
        ),
    )(
        velocity,
        jnp.transpose(profile, (1, 0, 2)),
        normal,
        height.reshape(TILES, TILE),
        pressure_grad,
        owner_device.reshape(TILES, TILE),
        match_cell.reshape(TILES, TILE),
    )
    return new_velocity, jnp.transpose(wall_profile, (1, 0, 2)), wall_stress


def solution(mesh):
    return jax.shard_map(
        per_device,
        mesh=mesh,
        in_specs=(
            P(None, "slab", "span", None),
            P(None, None, ("slab", "span")),
            P(None, ("slab", "span")),
            P(("slab", "span")),
            P(None, ("slab", "span")),
            P(("slab", "span"), None),
            P(("slab", "span")),
        ),
        out_specs=(
            P(None, "slab", "span", None),
            P(None, None, ("slab", "span")),
            P(None, ("slab", "span")),
        ),
        check_vma=False,
    )
```

```python
import jax
import jax.numpy as jnp
import numpy as np
from jax import lax
from jax.experimental import pallas as pl
from jax.experimental.pallas import tpu as pltpu
from jax.sharding import PartitionSpec as P

MESH = pl.DeviceIdType.MESH
BF16, F32, I32 = jnp.bfloat16, jnp.float32, jnp.int32

DEVICES = 128
SLOTS = 32
TILE = 128
TILES = 16
LEVELS = 32
CX, CY, ZB = 8, 32, 4
XY = CX * CY
NZ = 512
TOP = 8
MIB = 1 << 20
EARLY = 5

time_step = 0.1
viscosity = 0.001
smag_coef = 0.02
kappa_coef = 0.41
damping_plus = 26.0
stretch = 1.12
area_ratio = 4.0

FRAC = (stretch ** np.arange(LEVELS + 2) - 1.0) / (stretch ** (LEVELS + 1) - 1.0)
SPACING = FRAC[1:] - FRAC[:-1]
FACE = 0.5 * (FRAC[1:] + FRAC[:-1])
SPAN = 0.5 * (FRAC[2:] - FRAC[:-2])
LOWER = [float(v) for v in time_step / (SPACING[:-1] * SPAN)]
UPPER = [float(v) for v in time_step / (SPACING[1:] * SPAN)]


def dot_nn(a, b):
    return lax.dot_general(a, b, (((1,), (0,)), ((), ())), preferred_element_type=F32)


def dot_nt(a, b):
    return lax.dot_general(a, b, (((1,), (1,)), ((), ())), preferred_element_type=F32)


def split(value):
    high = value.astype(BF16)
    return high, (value - high.astype(F32)).astype(BF16)


def columns(j):
    return pl.ds(j * TILE, TILE)


def build_request(owner, cell, onehot, rank, picked, message):
    rows = lax.broadcasted_iota(I32, (TILE, TILE), 0)
    lanes = lax.broadcasted_iota(I32, (TILE, TILE), 1)
    earlier = jnp.where(rows < lanes, 1.0, 0.0).astype(BF16)
    summing = jnp.concatenate([earlier, jnp.ones((TILE, TILE), BF16)], axis=1)
    slots = lax.broadcasted_iota(I32, (SLOTS, TILE), 0)
    picked[3 * SLOTS :, :] = jnp.zeros((SLOTS, TILES * TILE), BF16)
    taken = jnp.zeros((TILE, TILE), F32)
    for j in range(TILES):
        mine = rows == owner[j : j + 1, :]
        one = jnp.where(mine, 1.0, 0.0).astype(BF16)
        onehot[:, columns(j)] = one
        counts = dot_nn(one, summing)
        place = jnp.sum(jnp.where(mine, counts[:, :TILE] + taken, 0.0), axis=0, keepdims=True).astype(I32)
        taken = taken + counts[:, TILE:]
        rank[j : j + 1, :] = place
        at = cell[j : j + 1, :]
        slot = slots == place
        depth = at & (NZ - 1)
        for part, value in enumerate((at >> 9, depth & (NZ - 2), depth & 1)):
            picked[part * SLOTS : (part + 1) * SLOTS, columns(j)] = jnp.where(slot, value.astype(F32), 0.0).astype(BF16)
    message[:, 0, :] = dot_nt(onehot[...], picked[...])


def read_request(arrived, request):
    turned = arrived[:, 0, :].T
    request[0:SLOTS, :] = turned[0:SLOTS].astype(I32)
    request[SLOTS : 2 * SLOTS, :] = (turned[SLOTS : 2 * SLOTS] + turned[2 * SLOTS : 3 * SLOTS]).astype(I32)


def gather_cells(request, v_high, v_low, gathered, begin, end):
    depths = lax.broadcasted_iota(I32, (NZ, TILE), 0)
    planes = lax.broadcasted_iota(I32, (XY, TILE), 0)

    @pl.loop(begin, end)
    def _(pair):
        hots = []
        for half in range(2):
            slot = pair * 2 + half
            row = request[pl.ds(SLOTS + slot, 1), :]
            hots.append(jnp.where(depths == row, 1.0, 0.0).astype(BF16))
        hot = jnp.concatenate(hots, axis=1)
        for c in range(3):
            part = pl.ds(c * XY, XY)
            found = dot_nn(v_high[part, :], hot) + dot_nn(v_low[part, :], hot)
            for half in range(2):
                slot = pair * 2 + half
                where = planes == request[pl.ds(slot, 1), :]
                gathered[pl.ds(c * SLOTS + slot, 1), :] = jnp.sum(
                    jnp.where(where, found[:, half * TILE : (half + 1) * TILE], 0.0), axis=0, keepdims=True
                )


def scatter_kernel(requests, stresses, base, wall_in, stress_in, out, wall_out, stress_out, depth_hot, pushes, planes_of):
    c = pl.program_id(0)
    wall_out[...] = wall_in[...]

    @pl.when(c == 0)
    def _():
        stress_out[...] = stress_in[...]
        pushes[...] = stresses[...].T
        planes_of[...] = requests[...].T[0:SLOTS]
        depths = lax.broadcasted_iota(I32, (TILE, NZ), 1)
        depth = (requests[:, SLOTS : 2 * SLOTS] + requests[:, 2 * SLOTS : 3 * SLOTS]).astype(I32)
        for slot in range(SLOTS):
            hot = jnp.where(depths == depth[:, slot : slot + 1], 1.0, 0.0).astype(BF16)
            depth_hot[slot // 2, columns(slot % 2), :] = hot

    planes = lax.broadcasted_iota(I32, (XY, TILE), 0).astype(F32).astype(BF16)
    zero = jnp.zeros((), BF16)
    total = jnp.zeros((XY, NZ), F32)
    for pair in range(SLOTS // 2):
        highs, lows = [], []
        for slot in (2 * pair, 2 * pair + 1):
            high, low = split(pushes[pl.ds(c * SLOTS + slot, 1), :])
            where = planes == planes_of[slot : slot + 1, :].astype(BF16)
            highs.append(jnp.where(where, high, zero))
            lows.append(jnp.where(where, low, zero))
        for part in (highs, lows):
            total = total + dot_nn(jnp.concatenate(part, axis=1), depth_hot[pair])
    for x in range(CX):
        out[0, x] = base[0, x] + total[x * CY : (x + 1) * CY]


def prepare(field, v_high, v_low):
    @pl.loop(0, 3 * CX)
    def _(i):
        c, x = i // CX, i % CX
        for zb in range(ZB):
            high, low = split(field[c, x + 1, zb, TOP : TOP + CY, :])
            rows = pl.ds(pl.multiple_of(i * CY, CY), CY)
            v_high[rows, columns(zb)] = high
            v_low[rows, columns(zb)] = low


def pack_rows(field, edge):
    for side, row in ((0, TOP), (1, TOP + CY - 1)):
        for c in range(3):
            for x in range(CX):
                edge[side, c * CX + x] = field[c, x + 1, :, row, :]


def unpack_rows(field, edge, span, spans):
    for side, row in ((0, TOP - 1), (1, TOP + CY)):
        for c in range(3):
            for x in range(CX):
                field[c, x + 1, :, row, :] = edge[side, c * CX + x]
    zero_row = jnp.zeros((CX, ZB, TILE), F32)
    for at, row in ((0, TOP - 1), (spans - 1, TOP + CY)):

        @pl.when(span == at)
        def _():
            for c in range(3):
                field[c, 1 : CX + 1, :, row, :] = zero_row


def clear_planes(field, slab, slabs):
    zero_plane = jnp.zeros((ZB, CY, TILE), F32)
    for at, plane in ((0, 0), (slabs - 1, CX + 1)):

        @pl.when(slab == at)
        def _():
            for c in range(3):
                field[c, plane, :, TOP : TOP + CY, :] = zero_plane


def stage(field, first, store, keep, mix, planes):
    lane = lax.broadcasted_iota(I32, (8, TILE), 1)
    at_start, at_end = lane == 0, lane == TILE - 1
    zeros = jnp.zeros((8, TILE), F32)

    @pl.loop(0, len(planes))
    def _(i):
        x = planes.start + i * planes.step
        for y in range(0, CY, 8):
            here = pl.ds(TOP + y, 8)
            center = [[field[c, x + 1, zb, here, :] for zb in range(ZB)] for c in range(3)]
            ahead = [[pltpu.roll(v, TILE - 1, 1) for v in row] for row in center]
            behind = [[pltpu.roll(v, 1, 1) for v in row] for row in center]
            for zb in range(ZB):
                mid = [center[c][zb] for c in range(3)]
                shear = zeros
                lap, grads = [], []
                for c in range(3):
                    xp, xm = field[c, x + 2, zb, here, :], field[c, x, zb, here, :]
                    yp, ym = field[c, x + 1, zb, pl.ds(TOP + y + 1, 8), :], field[c, x + 1, zb, pl.ds(TOP + y - 1, 8), :]
                    zp = jnp.where(at_end, ahead[c][zb + 1] if zb + 1 < ZB else zeros, ahead[c][zb])
                    zm = jnp.where(at_start, behind[c][zb - 1] if zb else zeros, behind[c][zb])
                    gx, gy, gz = xp - xm, yp - ym, zp - zm
                    shear = shear + (gx * gx + gy * gy + gz * gz)
                    lap.append(((xp + xm) + (yp + ym)) + ((zp + zm) - 6.0 * mid[c]))
                    grads.append(mid[0] * gx + mid[1] * gy + mid[2] * gz)
                eddy = viscosity + (0.5 * smag_coef) * jnp.sqrt(shear)
                for c in range(3):
                    moved = mid[c] + time_step * (eddy * lap[c] - 0.5 * grads[c])
                    if keep:
                        moved = keep * first[c, x + 1, zb, here, :] + mix * moved
                    store(c, x, y, zb, moved)


def tangential(vector, normal):
    along = vector[0] * normal[0] + vector[1] * normal[1] + vector[2] * normal[2]
    return [vector[c] - along * normal[c] for c in range(3)]


def level(ref, c, k):
    return ref[c, pl.ds(k, TILES, stride=LEVELS), :]


def diffusivity(first, height, inverse2):
    ratio = float((viscosity / FRAC[1]) ** 2)
    square = (first[0] * first[0] + first[1] * first[1] + first[2] * first[2]) * inverse2 * ratio
    scaled = height * jnp.sqrt(jnp.sqrt(square))

    def at(k):
        damping = 1.0 - jnp.exp(scaled * float(-FACE[k] / (viscosity * damping_plus)))
        return viscosity + (float(kappa_coef * FACE[k]) * scaled) * (damping * damping)

    return at


def sweep_one(profile, height, inverse2, forcing, kept):
    at = diffusivity([level(profile, c, 0) for c in range(3)], height, inverse2)
    above = at(LEVELS)
    ratio = jnp.zeros((TILES, TILE), F32)
    value = [jnp.zeros((TILES, TILE), F32)] * 3
    answer = jnp.ones((TILES, TILE), F32)
    for k in range(LEVELS - 1, -1, -1):
        below = at(k)
        low = (below * inverse2) * LOWER[k]
        up = (above * inverse2) * UPPER[k]
        inverse = 1.0 / (1.0 + low + up * (1.0 - ratio))
        ratio = low * inverse
        value = [(level(profile, c, k) - time_step * forcing[c] + up * value[c]) * inverse for c in range(3)]
        answer = answer * (up * inverse)
        above = below
    for c in range(3):
        kept[c] = value[c]
    kept[3] = answer


def sweep_two(profile, height, inverse2, forcing, target, kept, ratios, values):
    at = diffusivity([kept[c] + kept[3] * target[c] for c in range(3)], height, inverse2)
    above = at(LEVELS)
    ratio = jnp.zeros((TILES, TILE), F32)
    value = target
    for k in range(LEVELS - 1, -1, -1):
        below = at(k)
        low = (below * inverse2) * LOWER[k]
        up = (above * inverse2) * UPPER[k]
        inverse = 1.0 / (1.0 + low + up * (1.0 - ratio))
        ratio = low * inverse
        ratios[k] = ratio
        value = [(level(profile, c, k) - time_step * forcing[c] + up * value[c]) * inverse for c in range(3)]
        for c in range(3):
            values[c, k] = value[c]
        above = below
    return value


def substitute(ratios, values, result):
    value = [values[c, 0] for c in range(3)]
    for k in range(LEVELS):
        if k:
            value = [values[c, k] + ratios[k] * value[c] for c in range(3)]
        for c in range(3):
            result[c, pl.ds(k, TILES, stride=LEVELS), :] = value[c]


def take_matched(arrived, onehot, rank, matched):
    high, low = split(arrived[:, 0, :].T)
    slots = lax.broadcasted_iota(I32, (SLOTS, TILE), 0)
    for j in range(TILES):
        one = onehot[:, columns(j)]
        found = dot_nn(high, one) + dot_nn(low, one)
        slot = slots == rank[j : j + 1, :]
        for c in range(3):
            matched[c, j : j + 1, :] = jnp.sum(
                jnp.where(slot, found[c * SLOTS : (c + 1) * SLOTS], 0.0), axis=0, keepdims=True
            )


def send_stress(stress, onehot, rank, picked, picked_low, message):
    picked_low[3 * SLOTS :, :] = jnp.zeros((SLOTS, TILES * TILE), BF16)
    slots = lax.broadcasted_iota(I32, (SLOTS, TILE), 0)
    for j in range(TILES):
        slot = slots == rank[j : j + 1, :]
        for c in range(3):
            push = (-time_step * area_ratio) * stress[c, j : j + 1, :]
            high = push.astype(BF16).astype(F32)
            rows = slice(c * SLOTS, (c + 1) * SLOTS)
            picked[rows, columns(j)] = jnp.where(slot, high, 0.0).astype(BF16)
            picked_low[rows, columns(j)] = jnp.where(slot, push - high, 0.0).astype(BF16)
    message[:, 0, :] = dot_nt(onehot[...], picked[...]) + dot_nt(onehot[...], picked_low[...])


def kernel(
    velocity, profile_in, normal_in, height_in, pressure_in, owner_in, cell_in,
    stepped_out, wall_profile, wall_stress, requests, stresses,
    field_0, field_1, field_2, stepped, v_high, v_low,
    onehot, rank, picked, picked_low, request, gathered,
    profile, result, ratios, values, vectors, kept,
    owner, cell, height_v, normal_v, pressure_v,
    outgoing, incoming, edge_out, edge_in,
    small_sem, load_sem, profile_sem, store_sem, row_send, row_recv, halo_send, halo_recv,
):
    slab, span = lax.axis_index("slab"), lax.axis_index("span")
    slabs, spans = 16, 8
    me = slab * spans + span
    fields = (field_0, field_1, field_2)
    barrier = pltpu.get_barrier_semaphore()

    small = [
        pltpu.make_async_copy(src, dst, small_sem.at[i])
        for i, (src, dst) in enumerate(
            ((owner_in, owner), (cell_in, cell), (height_in, height_v), (normal_in, normal_v), (pressure_in, pressure_v))
        )
    ]
    for copy in small:
        copy.start()

    @pl.loop(0, slabs)
    def _(i):
        to = lax.rem(slab + i, slabs)
        for j in range(1, spans):
            pl.semaphore_signal(barrier, 1, device_id=(to, lax.rem(span + j, spans)), device_id_type=MESH)

    @pl.loop(1, slabs)
    def _(i):
        pl.semaphore_signal(barrier, 1, device_id=(lax.rem(slab + i, slabs), span), device_id_type=MESH)

    loads = [
        pltpu.make_async_copy(
            velocity.at[:, :, :, columns(zb)], field_0.at[:, pl.ds(1, CX), zb, pl.ds(TOP, CY), :], load_sem.at[zb]
        )
        for zb in range(ZB)
    ]
    for copy in loads:
        copy.start()
    profile_loads = [
        pltpu.make_async_copy(
            profile_in.at[:, :, columns(j)], profile.at[:, pl.ds(j * LEVELS, LEVELS), :], profile_sem.at[j]
        )
        for j in range(TILES)
    ]
    for copy in profile_loads:
        copy.start()

    arrivals = (incoming.at[0], incoming.at[1], stresses)

    def send_row(phase, to_slab, to_span):
        pltpu.make_async_remote_copy(
            src_ref=outgoing.at[phase, to_slab * spans + to_span],
            dst_ref=arrivals[phase].at[me],
            send_sem=row_send.at[phase],
            recv_sem=row_recv.at[phase],
            device_id=(to_slab, to_span),
            device_id_type=MESH,
        ).start()

    def send_rows(phase):
        for across in (2, 1, 3, 0):

            @pl.loop(1 if across == 0 else 0, 4)
            def _(i):
                to = lax.rem(slab + across * 4 + i, slabs)
                for j in range(spans):
                    send_row(phase, to, lax.rem(span + j, spans))

        for j in range(1, spans):
            send_row(phase, slab, lax.rem(span + j, spans))
        if phase < 2:
            incoming[phase, me] = outgoing[phase, me]

    def await_rows(phase):
        rows = outgoing.at[phase, pl.ds(0, DEVICES - 1)]
        pltpu.make_async_copy(rows, rows, row_send.at[phase]).wait()
        rows = arrivals[phase].at[pl.ds(0, DEVICES - 1)]
        pltpu.make_async_copy(rows, rows, row_recv.at[phase]).wait()

    up_x = (lax.rem(slab + 1, slabs), span)
    down_x = (lax.rem(slab + slabs - 1, slabs), span)
    up_y = (slab, lax.rem(span + 1, spans))
    down_y = (slab, lax.rem(span + spans - 1, spans))

    def send_halo(n):
        field = fields[n]
        inner = pl.ds(TOP, CY)
        ends = (
            (field.at[:, CX, :, inner, :], field.at[:, 0, :, inner, :], up_x),
            (field.at[:, 1, :, inner, :], field.at[:, CX + 1, :, inner, :], down_x),
            (edge_out.at[n, 1], edge_in.at[n, 0], up_y),
            (edge_out.at[n, 0], edge_in.at[n, 1], down_y),
        )
        copies = [
            pltpu.make_async_remote_copy(
                src_ref=src, dst_ref=dst, send_sem=halo_send.at[n, i], recv_sem=halo_recv.at[n, i],
                device_id=to, device_id_type=MESH,
            )
            for i, (src, dst, to) in enumerate(ends)
        ]
        for copy in copies[:2]:
            copy.start()
        pack_rows(field, edge_out.at[n])
        for copy in copies[2:]:
            copy.start()
        return copies

    def await_y(n, copies):
        for copy in copies[2:]:
            copy.wait()
        unpack_rows(fields[n], edge_in.at[n], span, spans)

    def await_x(n, copies):
        for copy in copies[:2]:
            copy.wait()
        clear_planes(fields[n], slab, slabs)

    def into(field):
        def store(c, x, y, zb, value):
            field[c, x + 1, zb, pl.ds(TOP + y, 8), :] = value

        return store

    def into_result(c, x, y, zb, value):
        stepped[c, x, zb, pl.ds(y, 8), :] = value

    for copy in small[:2]:
        copy.wait()
    build_request(owner, cell, onehot, rank, picked, outgoing.at[0])
    for copy in loads:
        copy.wait()
    pl.semaphore_wait(barrier, DEVICES - 1)
    send_rows(0)
    copies = send_halo(0)

    for copy in small[2:] + profile_loads:
        copy.wait()
    normal, pressure, matched = vectors.at[0], vectors.at[1], vectors.at[2]
    for c in range(3):
        for j in range(TILES):
            normal[c, j : j + 1, :] = normal_v[c : c + 1, columns(j)]
            pressure[c, j : j + 1, :] = pressure_v[c : c + 1, columns(j)]
    height = height_v[...]
    inverse2 = 1.0 / (height * height)
    forcing = tangential([pressure[c] for c in range(3)], [normal[c] for c in range(3)])
    sweep_one(profile, height, inverse2, forcing, kept)
    prepare(field_0, v_high, v_low)
    await_y(0, copies)
    stage(field_0, field_0, into(field_1), None, None, range(1, CX - 1))

    await_rows(0)
    read_request(incoming.at[0], request)
    keep_requests = pltpu.make_async_copy(incoming.at[0], requests, store_sem.at[0])
    keep_requests.start()
    gather_cells(request, v_high, v_low, gathered, 0, EARLY)
    await_x(0, copies)
    stage(field_0, field_0, into(field_1), None, None, range(0, CX, CX - 1))
    copies = send_halo(1)
    gather_cells(request, v_high, v_low, gathered, EARLY, SLOTS // 2)
    outgoing[1, :, 0, :] = gathered[...].T
    send_rows(1)

    await_y(1, copies)
    await_x(1, copies)
    stage(field_1, field_0, into(field_2), 0.75, 0.25, range(0, CX))
    copies = send_halo(2)

    await_rows(1)
    take_matched(incoming.at[1], onehot, rank, matched)
    target = tangential([matched[c] for c in range(3)], [normal[c] for c in range(3)])
    forcing = tangential([pressure[c] for c in range(3)], [normal[c] for c in range(3)])
    first = sweep_two(profile, height, inverse2, forcing, target, kept, ratios, values)
    scale = float(viscosity / FRAC[1]) / height
    stress = vectors.at[3]
    for c in range(3):
        stress[c] = first[c] * scale
    send_stress(stress, onehot, rank, picked, picked_low, outgoing.at[2])
    send_rows(2)
    own_row = pltpu.make_async_copy(outgoing.at[2, me], stresses.at[me], store_sem.at[1])
    own_row.start()

    for c in range(3):
        for j in range(TILES):
            wall_stress[c : c + 1, columns(j)] = stress[c, j : j + 1, :]
    await_y(2, copies)
    await_x(2, copies)
    stage(field_2, field_0, into_result, 1.0 / 3.0, 2.0 / 3.0, range(0, CX))
    stores = [
        pltpu.make_async_copy(stepped.at[:, :, zb], stepped_out.at[:, :, :, columns(zb)], load_sem.at[zb])
        for zb in range(ZB)
    ]
    for copy in stores:
        copy.start()
    substitute(ratios, values, result)
    profile_stores = [
        pltpu.make_async_copy(
            result.at[:, pl.ds(j * LEVELS, LEVELS), :], wall_profile.at[:, :, columns(j)], profile_sem.at[j]
        )
        for j in range(TILES)
    ]
    for copy in profile_stores:
        copy.start()
    for copy in [keep_requests, own_row] + stores + profile_stores:
        copy.wait()
    await_rows(2)


def per_device(velocity, profile, normal, height, pressure_grad, owner_device, match_cell):
    padded = pltpu.VMEM((3, CX + 2, ZB, CY + 16, TILE), F32)
    hbm, vmem = pl.BlockSpec(memory_space=pltpu.HBM), pl.BlockSpec(memory_space=pltpu.VMEM)
    wall_shape = jax.ShapeDtypeStruct((3, LEVELS, TILES * TILE), F32)
    stress_shape = jax.ShapeDtypeStruct((3, TILES * TILE), F32)
    rows_shape = jax.ShapeDtypeStruct((DEVICES, 1, TILE), F32)
    stepped, wall_profile, wall_stress, requests, stresses = pl.pallas_call(
        kernel,
        out_shape=(jax.ShapeDtypeStruct(velocity.shape, F32), wall_shape, stress_shape, rows_shape, rows_shape),
        in_specs=[hbm] * 7,
        out_specs=(hbm, hbm, vmem, hbm, hbm),
        scratch_shapes=[
            padded, padded, padded,
            pltpu.VMEM((3, CX, ZB, CY, TILE), F32),
            pltpu.VMEM((3 * XY, NZ), BF16), pltpu.VMEM((3 * XY, NZ), BF16),
            pltpu.VMEM((DEVICES, TILES * TILE), BF16),
            pltpu.VMEM((TILES, TILE), I32),
            pltpu.VMEM((DEVICES, TILES * TILE), BF16), pltpu.VMEM((DEVICES, TILES * TILE), BF16),
            pltpu.VMEM((2 * SLOTS, TILE), I32),
            pltpu.VMEM((DEVICES, TILE), F32),
            pltpu.VMEM((3, TILES * LEVELS, TILE), F32), pltpu.VMEM((3, TILES * LEVELS, TILE), F32),
            pltpu.VMEM((LEVELS, TILES, TILE), F32), pltpu.VMEM((3, LEVELS, TILES, TILE), F32),
            pltpu.VMEM((4, 3, TILES, TILE), F32), pltpu.VMEM((4, TILES, TILE), F32),
            pltpu.VMEM((TILES, TILE), I32), pltpu.VMEM((TILES, TILE), I32), pltpu.VMEM((TILES, TILE), F32),
            pltpu.VMEM((3, TILES * TILE), F32), pltpu.VMEM((3, TILES * TILE), F32),
            pltpu.VMEM((3, DEVICES, 1, TILE), F32), pltpu.VMEM((3, DEVICES, 1, TILE), F32),
            pltpu.VMEM((3, 2, 3 * CX, ZB, TILE), F32), pltpu.VMEM((3, 2, 3 * CX, ZB, TILE), F32),
            pltpu.SemaphoreType.DMA((5,)), pltpu.SemaphoreType.DMA((ZB,)), pltpu.SemaphoreType.DMA((TILES,)), pltpu.SemaphoreType.DMA((2,)),
            pltpu.SemaphoreType.DMA((3,)), pltpu.SemaphoreType.DMA((3,)),
            pltpu.SemaphoreType.DMA((3, 4)), pltpu.SemaphoreType.DMA((3, 4)),
        ],
        compiler_params=pltpu.CompilerParams(
            collective_id=0, has_side_effects=True, vmem_limit_bytes=60 * MIB
        ),
    )(
        velocity,
        jnp.transpose(profile, (1, 0, 2)),
        normal,
        height.reshape(TILES, TILE),
        pressure_grad,
        owner_device.reshape(TILES, TILE),
        match_cell.reshape(TILES, TILE),
    )
    plane = pl.BlockSpec((1, CX, CY, NZ), lambda c: (c, 0, 0, 0))
    walls = pl.BlockSpec((1, LEVELS, TILES * TILE), lambda c: (c, 0, 0))
    whole = pl.BlockSpec((DEVICES, TILE), lambda c: (0, 0))
    whole_stress = pl.BlockSpec((3, TILES * TILE), lambda c: (0, 0))
    new_velocity, wall_profile, wall_stress = pl.pallas_call(
        scatter_kernel,
        grid=(3,),
        out_shape=(jax.ShapeDtypeStruct(velocity.shape, F32), wall_shape, stress_shape),
        in_specs=[whole, whole, plane, walls, whole_stress],
        out_specs=(plane, walls, whole_stress),
        scratch_shapes=[
            pltpu.VMEM((SLOTS // 2, 2 * TILE, NZ), BF16),
            pltpu.VMEM((DEVICES, TILE), F32),
            pltpu.VMEM((SLOTS, TILE), F32),
        ],
        compiler_params=pltpu.CompilerParams(vmem_limit_bytes=60 * MIB),
    )(requests.reshape(DEVICES, TILE), stresses.reshape(DEVICES, TILE), stepped, wall_profile, wall_stress)
    return new_velocity, jnp.transpose(wall_profile, (1, 0, 2)), wall_stress


def solution(mesh):
    return jax.shard_map(
        per_device,
        mesh=mesh,
        in_specs=(
            P(None, "slab", "span", None),
            P(None, None, ("slab", "span")),
            P(None, ("slab", "span")),
            P(("slab", "span")),
            P(None, ("slab", "span")),
            P(("slab", "span"), None),
            P(("slab", "span")),
        ),
        out_specs=(
            P(None, "slab", "span", None),
            P(None, None, ("slab", "span")),
            P(None, ("slab", "span")),
        ),
        check_vma=False,
    )
```

```python
import jax
import jax.numpy as jnp
import numpy as np
from jax import lax
from jax.experimental import pallas as pl
from jax.experimental.pallas import tpu as pltpu
from jax.sharding import PartitionSpec as P

MESH = pl.DeviceIdType.MESH
BF16, F32, I32 = jnp.bfloat16, jnp.float32, jnp.int32

DEVICES = 128
SLOTS = 32
TILE = 128
TILES = 16
LEVELS = 32
CX, CY, ZB = 8, 32, 4
XY = CX * CY
NZ = 512
TOP = 8
MIB = 1 << 20
INNER, OUTER = range(1, CX - 1), range(0, CX, CX - 1)
EARLY = 6

time_step = 0.1
viscosity = 0.001
smag_coef = 0.02
kappa_coef = 0.41
damping_plus = 26.0
stretch = 1.12
area_ratio = 4.0

FRAC = (stretch ** np.arange(LEVELS + 2) - 1.0) / (stretch ** (LEVELS + 1) - 1.0)
SPACING = FRAC[1:] - FRAC[:-1]
FACE = 0.5 * (FRAC[1:] + FRAC[:-1])
SPAN = 0.5 * (FRAC[2:] - FRAC[:-2])
LOWER = [float(v) for v in time_step / (SPACING[:-1] * SPAN)]
UPPER = [float(v) for v in time_step / (SPACING[1:] * SPAN)]


def dot_nn(a, b):
    return lax.dot_general(a, b, (((1,), (0,)), ((), ())), preferred_element_type=F32)


def dot_nt(a, b):
    return lax.dot_general(a, b, (((1,), (1,)), ((), ())), preferred_element_type=F32)


def split(value):
    high = value.astype(BF16)
    return high, (value - high.astype(F32)).astype(BF16)


def columns(j):
    return pl.ds(j * TILE, TILE)


def build_request(owner, cell, onehot, rank, picked, message):
    rows = lax.broadcasted_iota(I32, (TILE, TILE), 0)
    lanes = lax.broadcasted_iota(I32, (TILE, TILE), 1)
    earlier = jnp.where(rows < lanes, 1.0, 0.0).astype(BF16)
    summing = jnp.concatenate([earlier, jnp.ones((TILE, TILE), BF16)], axis=1)
    slots = lax.broadcasted_iota(I32, (SLOTS, TILE), 0)
    picked[3 * SLOTS :, :] = jnp.zeros((SLOTS, TILES * TILE), BF16)
    taken = jnp.zeros((TILE, TILE), F32)
    for j in range(TILES):
        mine = rows == owner[j : j + 1, :]
        one = jnp.where(mine, 1.0, 0.0).astype(BF16)
        onehot[:, columns(j)] = one
        counts = dot_nn(one, summing)
        place = jnp.sum(jnp.where(mine, counts[:, :TILE] + taken, 0.0), axis=0, keepdims=True).astype(I32)
        taken = taken + counts[:, TILE:]
        rank[j : j + 1, :] = place
        at = cell[j : j + 1, :]
        slot = slots == place
        depth = at & (NZ - 1)
        for part, value in enumerate((at >> 9, depth & (NZ - 2), depth & 1)):
            picked[part * SLOTS : (part + 1) * SLOTS, columns(j)] = jnp.where(slot, value.astype(F32), 0.0).astype(BF16)
    message[:, 0, :] = dot_nt(onehot[...], picked[...])


def read_request(arrived, request):
    turned = arrived[:, 0, :].T
    request[0:SLOTS, :] = turned[0:SLOTS].astype(I32)
    request[SLOTS : 2 * SLOTS, :] = (turned[SLOTS : 2 * SLOTS] + turned[2 * SLOTS : 3 * SLOTS]).astype(I32)


def gather_cells(request, v_high, v_low, gathered, begin, end, step):
    depths = lax.broadcasted_iota(I32, (NZ, TILE), 0)
    planes = lax.broadcasted_iota(I32, (XY, TILE), 0)

    @pl.loop(begin, end, step=step)
    def _(first):
        for i in range(step):
            pair = first + i
            slots = (2 * pair, 2 * pair + 1)
            hots = [
                jnp.where(depths == request[pl.ds(SLOTS + slot, 1), :], 1.0, 0.0).astype(BF16) for slot in slots
            ]
            hot = jnp.concatenate(hots, axis=1)
            for c in range(3):
                part = slice(c * XY, (c + 1) * XY)
                found = dot_nn(v_high[part, :], hot) + dot_nn(v_low[part, :], hot)
                for half, slot in enumerate(slots):
                    where = planes == request[pl.ds(slot, 1), :]
                    gathered[pl.ds(c * SLOTS + slot, 1), :] = jnp.sum(
                        jnp.where(where, found[:, half * TILE : (half + 1) * TILE], 0.0), axis=0, keepdims=True
                    )


def scatter_kernel(requests, stresses, base, wall_in, stress_in, out, wall_out, stress_out, depth_hot, pushes, planes_of):
    c = pl.program_id(0)
    wall_out[...] = wall_in[...]

    @pl.when(c == 0)
    def _():
        stress_out[...] = stress_in[...]
        pushes[...] = stresses[...].T
        planes_of[...] = requests[...].T[0:SLOTS]
        depths = lax.broadcasted_iota(I32, (TILE, NZ), 1)
        depth = (requests[:, SLOTS : 2 * SLOTS] + requests[:, 2 * SLOTS : 3 * SLOTS]).astype(I32)
        for slot in range(SLOTS):
            hot = jnp.where(depths == depth[:, slot : slot + 1], 1.0, 0.0).astype(BF16)
            depth_hot[slot // 2, columns(slot % 2), :] = hot

    planes = lax.broadcasted_iota(I32, (XY, TILE), 0).astype(F32).astype(BF16)
    zero = jnp.zeros((), BF16)
    total = jnp.zeros((XY, NZ), F32)
    for pair in range(SLOTS // 2):
        highs, lows = [], []
        for slot in (2 * pair, 2 * pair + 1):
            high, low = split(pushes[pl.ds(c * SLOTS + slot, 1), :])
            where = planes == planes_of[slot : slot + 1, :].astype(BF16)
            highs.append(jnp.where(where, high, zero))
            lows.append(jnp.where(where, low, zero))
        for part in (highs, lows):
            total = total + dot_nn(jnp.concatenate(part, axis=1), depth_hot[pair])
    for x in range(CX):
        out[0, x] = base[0, x] + total[x * CY : (x + 1) * CY]


def prepare(field, v_high, v_low):
    @pl.loop(0, 3 * CX)
    def _(i):
        c, x = i // CX, i % CX
        for zb in range(ZB):
            high, low = split(field[c, x + 1, zb, TOP : TOP + CY, :])
            rows = pl.ds(pl.multiple_of(i * CY, CY), CY)
            v_high[rows, columns(zb)] = high
            v_low[rows, columns(zb)] = low


def pack_rows(field, edge):
    for side, row in ((0, TOP), (1, TOP + CY - 1)):
        for c in range(3):
            for x in range(CX):
                edge[side, c * CX + x] = field[c, x + 1, :, row, :]


def unpack_rows(field, edge, span, spans):
    for side, row in ((0, TOP - 1), (1, TOP + CY)):
        for c in range(3):
            for x in range(CX):
                field[c, x + 1, :, row, :] = edge[side, c * CX + x]
    zero_row = jnp.zeros((CX, ZB, TILE), F32)
    for at, row in ((0, TOP - 1), (spans - 1, TOP + CY)):

        @pl.when(span == at)
        def _():
            for c in range(3):
                field[c, 1 : CX + 1, :, row, :] = zero_row


def clear_planes(field, slab, slabs):
    zero_plane = jnp.zeros((ZB, CY, TILE), F32)
    for at, plane in ((0, 0), (slabs - 1, CX + 1)):

        @pl.when(slab == at)
        def _():
            for c in range(3):
                field[c, plane, :, TOP : TOP + CY, :] = zero_plane


def stage(field, first, store, keep, mix, planes):
    lane = lax.broadcasted_iota(I32, (8, TILE), 1)
    at_start, at_end = lane == 0, lane == TILE - 1
    zeros = jnp.zeros((8, TILE), F32)

    @pl.loop(0, len(planes))
    def _(i):
        x = planes.start + i * planes.step
        for y in range(0, CY, 8):
            here = pl.ds(TOP + y, 8)
            center = [[field[c, x + 1, zb, here, :] for zb in range(ZB)] for c in range(3)]
            ahead = [[pltpu.roll(v, TILE - 1, 1) for v in row] for row in center]
            behind = [[pltpu.roll(v, 1, 1) for v in row] for row in center]
            for zb in range(ZB):
                mid = [center[c][zb] for c in range(3)]
                shear = zeros
                lap, grads = [], []
                for c in range(3):
                    xp, xm = field[c, x + 2, zb, here, :], field[c, x, zb, here, :]
                    yp, ym = field[c, x + 1, zb, pl.ds(TOP + y + 1, 8), :], field[c, x + 1, zb, pl.ds(TOP + y - 1, 8), :]
                    zp = jnp.where(at_end, ahead[c][zb + 1] if zb + 1 < ZB else zeros, ahead[c][zb])
                    zm = jnp.where(at_start, behind[c][zb - 1] if zb else zeros, behind[c][zb])
                    gx, gy, gz = xp - xm, yp - ym, zp - zm
                    shear = shear + (gx * gx + gy * gy + gz * gz)
                    lap.append(((xp + xm) + (yp + ym)) + ((zp + zm) - 6.0 * mid[c]))
                    grads.append(mid[0] * gx + mid[1] * gy + mid[2] * gz)
                eddy = viscosity + (0.5 * smag_coef) * jnp.sqrt(shear)
                for c in range(3):
                    moved = mid[c] + time_step * (eddy * lap[c] - 0.5 * grads[c])
                    if keep:
                        moved = keep * first[c, x + 1, zb, here, :] + mix * moved
                    store(c, x, y, zb, moved)


def tangential(vector, normal):
    along = vector[0] * normal[0] + vector[1] * normal[1] + vector[2] * normal[2]
    return [vector[c] - along * normal[c] for c in range(3)]


def level(ref, c, k):
    return ref[c, pl.ds(k, TILES, stride=LEVELS), :]


def diffusivity(first, height, inverse2):
    ratio = float((viscosity / FRAC[1]) ** 2)
    square = (first[0] * first[0] + first[1] * first[1] + first[2] * first[2]) * inverse2 * ratio
    scaled = height * jnp.sqrt(jnp.sqrt(square))

    def at(k):
        damping = 1.0 - jnp.exp(scaled * float(-FACE[k] / (viscosity * damping_plus)))
        return viscosity + (float(kappa_coef * FACE[k]) * scaled) * (damping * damping)

    return at


def reciprocal(value):
    guess = pl.reciprocal(value, approx=True)
    return guess * (2.0 - value * guess)


def sweep_one(profile, height, inverse2, forcing, kept):
    at = diffusivity([level(profile, c, 0) for c in range(3)], height, inverse2)
    above = at(LEVELS)
    ratio = jnp.zeros((TILES, TILE), F32)
    value = [jnp.zeros((TILES, TILE), F32)] * 3
    answer = jnp.ones((TILES, TILE), F32)
    for k in range(LEVELS - 1, -1, -1):
        below = at(k)
        low = (below * inverse2) * LOWER[k]
        up = (above * inverse2) * UPPER[k]
        inverse = reciprocal(1.0 + low + up * (1.0 - ratio))
        ratio = low * inverse
        value = [(level(profile, c, k) - time_step * forcing[c] + up * value[c]) * inverse for c in range(3)]
        answer = answer * (up * inverse)
        above = below
    for c in range(3):
        kept[c] = value[c]
    kept[3] = answer


def sweep_two(profile, height, inverse2, forcing, target, kept, ratios, values):
    at = diffusivity([kept[c] + kept[3] * target[c] for c in range(3)], height, inverse2)
    above = at(LEVELS)
    ratio = jnp.zeros((TILES, TILE), F32)
    value = target
    for k in range(LEVELS - 1, -1, -1):
        below = at(k)
        low = (below * inverse2) * LOWER[k]
        up = (above * inverse2) * UPPER[k]
        inverse = reciprocal(1.0 + low + up * (1.0 - ratio))
        ratio = low * inverse
        ratios[k] = ratio
        value = [(level(profile, c, k) - time_step * forcing[c] + up * value[c]) * inverse for c in range(3)]
        for c in range(3):
            values[c, k] = value[c]
        above = below
    return value


def substitute(ratios, values, result):
    value = [values[c, 0] for c in range(3)]
    for k in range(LEVELS):
        if k:
            value = [values[c, k] + ratios[k] * value[c] for c in range(3)]
        for c in range(3):
            result[c, pl.ds(k, TILES, stride=LEVELS), :] = value[c]


def take_matched(arrived, onehot, rank, matched):
    high, low = split(arrived[:, 0, :].T)
    slots = lax.broadcasted_iota(I32, (SLOTS, TILE), 0)
    for j in range(TILES):
        one = onehot[:, columns(j)]
        found = dot_nn(high, one) + dot_nn(low, one)
        slot = slots == rank[j : j + 1, :]
        for c in range(3):
            matched[c, j : j + 1, :] = jnp.sum(
                jnp.where(slot, found[c * SLOTS : (c + 1) * SLOTS], 0.0), axis=0, keepdims=True
            )


def send_stress(stress, onehot, rank, picked, picked_low, message):
    picked_low[3 * SLOTS :, :] = jnp.zeros((SLOTS, TILES * TILE), BF16)
    slots = lax.broadcasted_iota(I32, (SLOTS, TILE), 0)
    for j in range(TILES):
        slot = slots == rank[j : j + 1, :]
        for c in range(3):
            push = (-time_step * area_ratio) * stress[c, j : j + 1, :]
            high = push.astype(BF16).astype(F32)
            rows = slice(c * SLOTS, (c + 1) * SLOTS)
            picked[rows, columns(j)] = jnp.where(slot, high, 0.0).astype(BF16)
            picked_low[rows, columns(j)] = jnp.where(slot, push - high, 0.0).astype(BF16)
    message[:, 0, :] = dot_nt(onehot[...], picked[...]) + dot_nt(onehot[...], picked_low[...])


def kernel(
    velocity, profile_in, normal_in, height_in, pressure_in, owner_in, cell_in,
    stepped_out, wall_profile, wall_stress, requests, stresses,
    field_0, field_1, field_2, stepped, v_high, v_low,
    onehot, rank, picked, picked_low, request, gathered,
    profile, result, ratios, values, vectors, kept,
    owner, cell, height_v, normal_v, pressure_v,
    outgoing, incoming, edge_out, edge_in,
    small_sem, load_sem, profile_sem, store_sem, plane_sem, row_send, row_recv, halo_send, halo_recv,
):
    slab, span = lax.axis_index("slab"), lax.axis_index("span")
    slabs, spans = 16, 8
    me = slab * spans + span
    fields = (field_0, field_1, field_2)
    barrier = pltpu.get_barrier_semaphore()

    small = [
        pltpu.make_async_copy(src, dst, small_sem.at[i])
        for i, (src, dst) in enumerate(
            ((owner_in, owner), (cell_in, cell), (height_in, height_v), (normal_in, normal_v), (pressure_in, pressure_v))
        )
    ]
    for copy in small:
        copy.start()

    @pl.loop(0, slabs)
    def _(i):
        to = lax.rem(slab + i, slabs)
        for j in range(1, spans):
            pl.semaphore_signal(barrier, 1, device_id=(to, lax.rem(span + j, spans)), device_id_type=MESH)

    @pl.loop(1, slabs)
    def _(i):
        pl.semaphore_signal(barrier, 1, device_id=(lax.rem(slab + i, slabs), span), device_id_type=MESH)

    loads = [
        pltpu.make_async_copy(
            velocity.at[:, :, :, columns(zb)], field_0.at[:, pl.ds(1, CX), zb, pl.ds(TOP, CY), :], load_sem.at[zb]
        )
        for zb in range(ZB)
    ]
    for copy in loads:
        copy.start()
    profile_loads = [
        pltpu.make_async_copy(
            profile_in.at[:, :, columns(j)], profile.at[:, pl.ds(j * LEVELS, LEVELS), :], profile_sem.at[j]
        )
        for j in range(TILES)
    ]
    for copy in profile_loads:
        copy.start()

    arrivals = (incoming.at[0], incoming.at[1], stresses)

    def send_row(phase, to_slab, to_span):
        pltpu.make_async_remote_copy(
            src_ref=outgoing.at[phase, to_slab * spans + to_span],
            dst_ref=arrivals[phase].at[me],
            send_sem=row_send.at[phase],
            recv_sem=row_recv.at[phase],
            device_id=(to_slab, to_span),
            device_id_type=MESH,
        ).start()

    def send_rows(phase):
        for across in (2, 1, 3, 0):

            @pl.loop(1 if across == 0 else 0, 4)
            def _(i):
                to = lax.rem(slab + across * 4 + i, slabs)
                for j in range(spans):
                    send_row(phase, to, lax.rem(span + j, spans))

        for j in range(1, spans):
            send_row(phase, slab, lax.rem(span + j, spans))
        if phase < 2:
            incoming[phase, me] = outgoing[phase, me]

    def await_rows(phase):
        rows = outgoing.at[phase, pl.ds(0, DEVICES - 1)]
        pltpu.make_async_copy(rows, rows, row_send.at[phase]).wait()
        rows = arrivals[phase].at[pl.ds(0, DEVICES - 1)]
        pltpu.make_async_copy(rows, rows, row_recv.at[phase]).wait()

    up_x = (lax.rem(slab + 1, slabs), span)
    down_x = (lax.rem(slab + slabs - 1, slabs), span)
    up_y = (slab, lax.rem(span + 1, spans))
    down_y = (slab, lax.rem(span + spans - 1, spans))

    def halo(n):
        field = fields[n]
        inner = pl.ds(TOP, CY)
        ends = (
            (field.at[:, CX, :, inner, :], field.at[:, 0, :, inner, :], up_x),
            (field.at[:, 1, :, inner, :], field.at[:, CX + 1, :, inner, :], down_x),
            (edge_out.at[n, 1], edge_in.at[n, 0], up_y),
            (edge_out.at[n, 0], edge_in.at[n, 1], down_y),
        )
        return [
            pltpu.make_async_remote_copy(
                src_ref=src, dst_ref=dst, send_sem=halo_send.at[n, i], recv_sem=halo_recv.at[n, i],
                device_id=to, device_id_type=MESH,
            )
            for i, (src, dst, to) in enumerate(ends)
        ]

    def send_x(copies):
        for copy in copies[:2]:
            copy.start()

    def send_y(n, copies):
        pack_rows(fields[n], edge_out.at[n])
        for copy in copies[2:]:
            copy.start()

    def await_y(n, copies):
        for copy in copies[2:]:
            copy.wait()
        unpack_rows(fields[n], edge_in.at[n], span, spans)

    def await_x(n, copies):
        for copy in copies[:2]:
            copy.wait()
        clear_planes(fields[n], slab, slabs)

    def into(field):
        def store(c, x, y, zb, value):
            field[c, x + 1, zb, pl.ds(TOP + y, 8), :] = value

        return store

    def into_result(c, x, y, zb, value):
        stepped[c, x, zb, pl.ds(y, 8), :] = value

    for copy in small[:2]:
        copy.wait()
    build_request(owner, cell, onehot, rank, picked, outgoing.at[0])
    for copy in loads:
        copy.wait()
    pl.semaphore_wait(barrier, DEVICES - 1)
    send_rows(0)
    copies = halo(0)
    send_y(0, copies)
    send_x(copies)

    for copy in small[2:] + profile_loads:
        copy.wait()
    normal, pressure, matched = vectors.at[0], vectors.at[1], vectors.at[2]
    for c in range(3):
        for j in range(TILES):
            normal[c, j : j + 1, :] = normal_v[c : c + 1, columns(j)]
            pressure[c, j : j + 1, :] = pressure_v[c : c + 1, columns(j)]
    height = height_v[...]
    inverse2 = 1.0 / (height * height)
    forcing = tangential([pressure[c] for c in range(3)], [normal[c] for c in range(3)])
    sweep_one(profile, height, inverse2, forcing, kept)
    prepare(field_0, v_high, v_low)
    await_y(0, copies)
    stage(field_0, field_0, into(field_1), None, None, INNER)

    await_rows(0)
    read_request(incoming.at[0], request)
    keep_requests = pltpu.make_async_copy(incoming.at[0], requests, store_sem.at[0])
    keep_requests.start()
    gather_cells(request, v_high, v_low, gathered, 0, EARLY, 3)
    await_x(0, copies)
    stage(field_0, field_0, into(field_1), None, None, OUTER)
    copies = halo(1)
    send_x(copies)
    send_y(1, copies)
    gather_cells(request, v_high, v_low, gathered, EARLY, SLOTS // 2, 5)
    outgoing[1, :, 0, :] = gathered[...].T
    send_rows(1)

    await_y(1, copies)
    stage(field_1, field_0, into(field_2), 0.75, 0.25, INNER)
    await_x(1, copies)
    stage(field_1, field_0, into(field_2), 0.75, 0.25, OUTER)
    copies = halo(2)
    send_x(copies)
    send_y(2, copies)

    await_rows(1)
    take_matched(incoming.at[1], onehot, rank, matched)
    target = tangential([matched[c] for c in range(3)], [normal[c] for c in range(3)])
    forcing = tangential([pressure[c] for c in range(3)], [normal[c] for c in range(3)])
    first = sweep_two(profile, height, inverse2, forcing, target, kept, ratios, values)
    scale = float(viscosity / FRAC[1]) / height
    stress = vectors.at[3]
    for c in range(3):
        stress[c] = first[c] * scale
    send_stress(stress, onehot, rank, picked, picked_low, outgoing.at[2])
    send_rows(2)
    own_row = pltpu.make_async_copy(outgoing.at[2, me], stresses.at[me], store_sem.at[1])
    own_row.start()

    for c in range(3):
        for j in range(TILES):
            wall_stress[c : c + 1, columns(j)] = stress[c, j : j + 1, :]
    def store_planes(number, begin, count):
        copies = [
            pltpu.make_async_copy(
                stepped.at[:, pl.ds(begin, count), zb],
                stepped_out.at[:, pl.ds(begin, count), :, columns(zb)],
                plane_sem.at[number, zb],
            )
            for zb in range(ZB)
        ]
        for copy in copies:
            copy.start()
        return copies

    await_y(2, copies)
    stage(field_2, field_0, into_result, 1.0 / 3.0, 2.0 / 3.0, INNER)
    stores = store_planes(0, 1, CX - 2)
    substitute(ratios, values, result)
    profile_stores = [
        pltpu.make_async_copy(
            result.at[:, pl.ds(j * LEVELS, LEVELS), :], wall_profile.at[:, :, columns(j)], profile_sem.at[j]
        )
        for j in range(TILES)
    ]
    for copy in profile_stores:
        copy.start()
    await_x(2, copies)
    stage(field_2, field_0, into_result, 1.0 / 3.0, 2.0 / 3.0, OUTER)
    stores += store_planes(1, 0, 1) + store_planes(2, CX - 1, 1)
    for copy in [keep_requests, own_row] + stores + profile_stores:
        copy.wait()
    await_rows(2)


def per_device(velocity, profile, normal, height, pressure_grad, owner_device, match_cell):
    padded = pltpu.VMEM((3, CX + 2, ZB, CY + 16, TILE), F32)
    hbm, vmem = pl.BlockSpec(memory_space=pltpu.HBM), pl.BlockSpec(memory_space=pltpu.VMEM)
    wall_shape = jax.ShapeDtypeStruct((3, LEVELS, TILES * TILE), F32)
    stress_shape = jax.ShapeDtypeStruct((3, TILES * TILE), F32)
    rows_shape = jax.ShapeDtypeStruct((DEVICES, 1, TILE), F32)
    stepped, wall_profile, wall_stress, requests, stresses = pl.pallas_call(
        kernel,
        out_shape=(jax.ShapeDtypeStruct(velocity.shape, F32), wall_shape, stress_shape, rows_shape, rows_shape),
        in_specs=[hbm] * 7,
        out_specs=(hbm, hbm, vmem, hbm, hbm),
        scratch_shapes=[
            padded, padded, padded,
            pltpu.VMEM((3, CX, ZB, CY, TILE), F32),
            pltpu.VMEM((3 * XY, NZ), BF16), pltpu.VMEM((3 * XY, NZ), BF16),
            pltpu.VMEM((DEVICES, TILES * TILE), BF16),
            pltpu.VMEM((TILES, TILE), I32),
            pltpu.VMEM((DEVICES, TILES * TILE), BF16), pltpu.VMEM((DEVICES, TILES * TILE), BF16),
            pltpu.VMEM((2 * SLOTS, TILE), I32),
            pltpu.VMEM((DEVICES, TILE), F32),
            pltpu.VMEM((3, TILES * LEVELS, TILE), F32), pltpu.VMEM((3, TILES * LEVELS, TILE), F32),
            pltpu.VMEM((LEVELS, TILES, TILE), F32), pltpu.VMEM((3, LEVELS, TILES, TILE), F32),
            pltpu.VMEM((4, 3, TILES, TILE), F32), pltpu.VMEM((4, TILES, TILE), F32),
            pltpu.VMEM((TILES, TILE), I32), pltpu.VMEM((TILES, TILE), I32), pltpu.VMEM((TILES, TILE), F32),
            pltpu.VMEM((3, TILES * TILE), F32), pltpu.VMEM((3, TILES * TILE), F32),
            pltpu.VMEM((3, DEVICES, 1, TILE), F32), pltpu.VMEM((3, DEVICES, 1, TILE), F32),
            pltpu.VMEM((3, 2, 3 * CX, ZB, TILE), F32), pltpu.VMEM((3, 2, 3 * CX, ZB, TILE), F32),
            pltpu.SemaphoreType.DMA((5,)), pltpu.SemaphoreType.DMA((ZB,)), pltpu.SemaphoreType.DMA((TILES,)), pltpu.SemaphoreType.DMA((2,)), pltpu.SemaphoreType.DMA((3, ZB)),
            pltpu.SemaphoreType.DMA((3,)), pltpu.SemaphoreType.DMA((3,)),
            pltpu.SemaphoreType.DMA((3, 4)), pltpu.SemaphoreType.DMA((3, 4)),
        ],
        compiler_params=pltpu.CompilerParams(
            collective_id=0, has_side_effects=True, vmem_limit_bytes=60 * MIB
        ),
    )(
        velocity,
        jnp.transpose(profile, (1, 0, 2)),
        normal,
        height.reshape(TILES, TILE),
        pressure_grad,
        owner_device.reshape(TILES, TILE),
        match_cell.reshape(TILES, TILE),
    )
    plane = pl.BlockSpec((1, CX, CY, NZ), lambda c: (c, 0, 0, 0))
    walls = pl.BlockSpec((1, LEVELS, TILES * TILE), lambda c: (c, 0, 0))
    whole = pl.BlockSpec((DEVICES, TILE), lambda c: (0, 0))
    whole_stress = pl.BlockSpec((3, TILES * TILE), lambda c: (0, 0))
    new_velocity, wall_profile, wall_stress = pl.pallas_call(
        scatter_kernel,
        grid=(3,),
        out_shape=(jax.ShapeDtypeStruct(velocity.shape, F32), wall_shape, stress_shape),
        in_specs=[whole, whole, plane, walls, whole_stress],
        out_specs=(plane, walls, whole_stress),
        scratch_shapes=[
            pltpu.VMEM((SLOTS // 2, 2 * TILE, NZ), BF16),
            pltpu.VMEM((DEVICES, TILE), F32),
            pltpu.VMEM((SLOTS, TILE), F32),
        ],
        compiler_params=pltpu.CompilerParams(vmem_limit_bytes=60 * MIB),
    )(requests.reshape(DEVICES, TILE), stresses.reshape(DEVICES, TILE), stepped, wall_profile, wall_stress)
    return new_velocity, jnp.transpose(wall_profile, (1, 0, 2)), wall_stress


def solution(mesh):
    return jax.shard_map(
        per_device,
        mesh=mesh,
        in_specs=(
            P(None, "slab", "span", None),
            P(None, None, ("slab", "span")),
            P(None, ("slab", "span")),
            P(("slab", "span")),
            P(None, ("slab", "span")),
            P(("slab", "span"), None),
            P(("slab", "span")),
        ),
        out_specs=(
            P(None, "slab", "span", None),
            P(None, None, ("slab", "span")),
            P(None, ("slab", "span")),
        ),
        check_vma=False,
    )
```

```python
import jax
import jax.numpy as jnp
import numpy as np
from jax import lax
from jax.experimental import pallas as pl
from jax.experimental.pallas import tpu as pltpu
from jax.sharding import PartitionSpec as P

MESH = pl.DeviceIdType.MESH
BF16, F32, I32 = jnp.bfloat16, jnp.float32, jnp.int32

DEVICES = 128
SLOTS = 32
TILE = 128
TILES = 16
LEVELS = 32
CX, CY, ZB = 8, 32, 4
XY = CX * CY
NZ = 512
TOP = 8
MIB = 1 << 20
INNER, OUTER = range(1, CX - 1), range(0, CX, CX - 1)
EARLY = 6

time_step = 0.1
viscosity = 0.001
smag_coef = 0.02
kappa_coef = 0.41
damping_plus = 26.0
stretch = 1.12
area_ratio = 4.0

FRAC = (stretch ** np.arange(LEVELS + 2) - 1.0) / (stretch ** (LEVELS + 1) - 1.0)
SPACING = FRAC[1:] - FRAC[:-1]
FACE = 0.5 * (FRAC[1:] + FRAC[:-1])
SPAN = 0.5 * (FRAC[2:] - FRAC[:-2])
LOWER = [float(v) for v in time_step / (SPACING[:-1] * SPAN)]
UPPER = [float(v) for v in time_step / (SPACING[1:] * SPAN)]


def dot_nn(a, b):
    return lax.dot_general(a, b, (((1,), (0,)), ((), ())), preferred_element_type=F32)


def dot_nt(a, b):
    return lax.dot_general(a, b, (((1,), (1,)), ((), ())), preferred_element_type=F32)


def split(value):
    high = value.astype(BF16)
    return high, (value - high.astype(F32)).astype(BF16)


def hops(offset):
    slab, span = offset
    return sum(min(step, 4 - step) for step in (slab // 4, slab % 4, span // 2)) + span % 2 / 2


FARTHEST_FIRST = sorted(((i, j) for i in range(16) for j in range(8) if i or j), key=hops, reverse=True)


def columns(j):
    return pl.ds(j * TILE, TILE)


def build_request(owner, cell, onehot, rank, picked, message):
    rows = lax.broadcasted_iota(I32, (TILE, TILE), 0)
    lanes = lax.broadcasted_iota(I32, (TILE, TILE), 1)
    earlier = jnp.where(rows < lanes, 1.0, 0.0).astype(BF16)
    summing = jnp.concatenate([earlier, jnp.ones((TILE, TILE), BF16)], axis=1)
    slots = lax.broadcasted_iota(I32, (SLOTS, TILE), 0)
    picked[3 * SLOTS :, :] = jnp.zeros((SLOTS, TILES * TILE), BF16)
    taken = jnp.zeros((TILE, TILE), F32)
    for j in range(TILES):
        mine = rows == owner[j : j + 1, :]
        one = jnp.where(mine, 1.0, 0.0).astype(BF16)
        onehot[:, columns(j)] = one
        counts = dot_nn(one, summing)
        place = jnp.sum(jnp.where(mine, counts[:, :TILE] + taken, 0.0), axis=0, keepdims=True).astype(I32)
        taken = taken + counts[:, TILE:]
        rank[j : j + 1, :] = place
        at = cell[j : j + 1, :]
        slot = slots == place
        depth = at & (NZ - 1)
        for part, value in enumerate((at >> 9, depth & (NZ - 2), depth & 1)):
            picked[part * SLOTS : (part + 1) * SLOTS, columns(j)] = jnp.where(slot, value.astype(F32), 0.0).astype(BF16)
    message[:, 0, :] = dot_nt(onehot[...], picked[...])


def read_request(arrived, request):
    turned = arrived[:, 0, :].T
    request[0:SLOTS, :] = turned[0:SLOTS].astype(I32)
    request[SLOTS : 2 * SLOTS, :] = (turned[SLOTS : 2 * SLOTS] + turned[2 * SLOTS : 3 * SLOTS]).astype(I32)


def gather_cells(request, v_high, v_low, gathered, begin, end, step):
    depths = lax.broadcasted_iota(I32, (NZ, TILE), 0)
    planes = lax.broadcasted_iota(I32, (XY, TILE), 0)

    @pl.loop(begin, end, step=step)
    def _(first):
        for i in range(step):
            pair = first + i
            slots = (2 * pair, 2 * pair + 1)
            hots = [
                jnp.where(depths == request[pl.ds(SLOTS + slot, 1), :], 1.0, 0.0).astype(BF16) for slot in slots
            ]
            hot = jnp.concatenate(hots, axis=1)
            for c in range(3):
                part = slice(c * XY, (c + 1) * XY)
                found = dot_nn(v_high[part, :], hot) + dot_nn(v_low[part, :], hot)
                for half, slot in enumerate(slots):
                    where = planes == request[pl.ds(slot, 1), :]
                    gathered[pl.ds(c * SLOTS + slot, 1), :] = jnp.sum(
                        jnp.where(where, found[:, half * TILE : (half + 1) * TILE], 0.0), axis=0, keepdims=True
                    )


def scatter_kernel(requests, stresses, base, wall_in, stress_in, out, wall_out, stress_out, depth_hot, pushes, planes_of):
    c = pl.program_id(0)
    wall_out[...] = wall_in[...]

    @pl.when(c == 0)
    def _():
        stress_out[...] = stress_in[...]
        pushes[...] = stresses[...].T
        planes_of[...] = requests[...].T[0:SLOTS]
        depths = lax.broadcasted_iota(I32, (TILE, NZ), 1)
        depth = (requests[:, SLOTS : 2 * SLOTS] + requests[:, 2 * SLOTS : 3 * SLOTS]).astype(I32)
        for slot in range(SLOTS):
            hot = jnp.where(depths == depth[:, slot : slot + 1], 1.0, 0.0).astype(BF16)
            depth_hot[slot // 2, columns(slot % 2), :] = hot

    planes = lax.broadcasted_iota(I32, (XY, TILE), 0).astype(F32).astype(BF16)
    zero = jnp.zeros((), BF16)
    total = jnp.zeros((XY, NZ), F32)
    for pair in range(SLOTS // 2):
        highs, lows = [], []
        for slot in (2 * pair, 2 * pair + 1):
            high, low = split(pushes[pl.ds(c * SLOTS + slot, 1), :])
            where = planes == planes_of[slot : slot + 1, :].astype(BF16)
            highs.append(jnp.where(where, high, zero))
            lows.append(jnp.where(where, low, zero))
        for part in (highs, lows):
            total = total + dot_nn(jnp.concatenate(part, axis=1), depth_hot[pair])
    for x in range(CX):
        out[0, x] = base[0, x] + total[x * CY : (x + 1) * CY]


def prepare(field, v_high, v_low):
    @pl.loop(0, 3 * CX)
    def _(i):
        c, x = i // CX, i % CX
        for zb in range(ZB):
            high, low = split(field[c, x + 1, zb, TOP : TOP + CY, :])
            rows = pl.ds(pl.multiple_of(i * CY, CY), CY)
            v_high[rows, columns(zb)] = high
            v_low[rows, columns(zb)] = low


def pack_rows(field, edge):
    for side, row in ((0, TOP), (1, TOP + CY - 1)):
        for c in range(3):
            for x in range(CX):
                edge[side, c * CX + x] = field[c, x + 1, :, row, :]


def unpack_rows(field, edge, span, spans):
    for side, row in ((0, TOP - 1), (1, TOP + CY)):
        for c in range(3):
            for x in range(CX):
                field[c, x + 1, :, row, :] = edge[side, c * CX + x]
    zero_row = jnp.zeros((CX, ZB, TILE), F32)
    for at, row in ((0, TOP - 1), (spans - 1, TOP + CY)):

        @pl.when(span == at)
        def _():
            for c in range(3):
                field[c, 1 : CX + 1, :, row, :] = zero_row


def clear_planes(field, slab, slabs):
    zero_plane = jnp.zeros((ZB, CY, TILE), F32)
    for at, plane in ((0, 0), (slabs - 1, CX + 1)):

        @pl.when(slab == at)
        def _():
            for c in range(3):
                field[c, plane, :, TOP : TOP + CY, :] = zero_plane


def stage(field, first, store, keep, mix, planes):
    lane = lax.broadcasted_iota(I32, (8, TILE), 1)
    at_start, at_end = lane == 0, lane == TILE - 1
    zeros = jnp.zeros((8, TILE), F32)

    @pl.loop(0, len(planes))
    def _(i):
        x = planes.start + i * planes.step
        for y in range(0, CY, 8):
            here = pl.ds(TOP + y, 8)
            center = [[field[c, x + 1, zb, here, :] for zb in range(ZB)] for c in range(3)]
            ahead = [[pltpu.roll(v, TILE - 1, 1) for v in row] for row in center]
            behind = [[pltpu.roll(v, 1, 1) for v in row] for row in center]
            for zb in range(ZB):
                mid = [center[c][zb] for c in range(3)]
                shear = zeros
                lap, grads = [], []
                for c in range(3):
                    xp, xm = field[c, x + 2, zb, here, :], field[c, x, zb, here, :]
                    yp, ym = field[c, x + 1, zb, pl.ds(TOP + y + 1, 8), :], field[c, x + 1, zb, pl.ds(TOP + y - 1, 8), :]
                    zp = jnp.where(at_end, ahead[c][zb + 1] if zb + 1 < ZB else zeros, ahead[c][zb])
                    zm = jnp.where(at_start, behind[c][zb - 1] if zb else zeros, behind[c][zb])
                    gx, gy, gz = xp - xm, yp - ym, zp - zm
                    shear = shear + (gx * gx + gy * gy + gz * gz)
                    lap.append(((xp + xm) + (yp + ym)) + ((zp + zm) - 6.0 * mid[c]))
                    grads.append(mid[0] * gx + mid[1] * gy + mid[2] * gz)
                eddy = viscosity + (0.5 * smag_coef) * jnp.sqrt(shear)
                for c in range(3):
                    moved = mid[c] + time_step * (eddy * lap[c] - 0.5 * grads[c])
                    if keep:
                        moved = keep * first[c, x + 1, zb, here, :] + mix * moved
                    store(c, x, y, zb, moved)


def tangential(vector, normal):
    along = vector[0] * normal[0] + vector[1] * normal[1] + vector[2] * normal[2]
    return [vector[c] - along * normal[c] for c in range(3)]


def level(ref, c, k):
    return ref[c, pl.ds(k, TILES, stride=LEVELS), :]


def diffusivity(first, height, inverse2):
    ratio = float((viscosity / FRAC[1]) ** 2)
    square = (first[0] * first[0] + first[1] * first[1] + first[2] * first[2]) * inverse2 * ratio
    scaled = height * jnp.sqrt(jnp.sqrt(square))

    def at(k):
        damping = 1.0 - jnp.exp(scaled * float(-FACE[k] / (viscosity * damping_plus)))
        return viscosity + (float(kappa_coef * FACE[k]) * scaled) * (damping * damping)

    return at


def reciprocal(value):
    guess = pl.reciprocal(value, approx=True)
    return guess * (2.0 - value * guess)


def sweep_one(profile, height, inverse2, forcing, kept):
    at = diffusivity([level(profile, c, 0) for c in range(3)], height, inverse2)
    above = at(LEVELS)
    ratio = jnp.zeros((TILES, TILE), F32)
    value = [jnp.zeros((TILES, TILE), F32)] * 3
    answer = jnp.ones((TILES, TILE), F32)
    for k in range(LEVELS - 1, -1, -1):
        below = at(k)
        low = (below * inverse2) * LOWER[k]
        up = (above * inverse2) * UPPER[k]
        inverse = reciprocal(1.0 + low + up * (1.0 - ratio))
        ratio = low * inverse
        value = [(level(profile, c, k) - time_step * forcing[c] + up * value[c]) * inverse for c in range(3)]
        answer = answer * (up * inverse)
        above = below
    for c in range(3):
        kept[c] = value[c]
    kept[3] = answer


def sweep_two(profile, height, inverse2, forcing, target, kept, ratios, values):
    at = diffusivity([kept[c] + kept[3] * target[c] for c in range(3)], height, inverse2)
    above = at(LEVELS)
    ratio = jnp.zeros((TILES, TILE), F32)
    value = target
    for k in range(LEVELS - 1, -1, -1):
        below = at(k)
        low = (below * inverse2) * LOWER[k]
        up = (above * inverse2) * UPPER[k]
        inverse = reciprocal(1.0 + low + up * (1.0 - ratio))
        ratio = low * inverse
        ratios[k] = ratio
        value = [(level(profile, c, k) - time_step * forcing[c] + up * value[c]) * inverse for c in range(3)]
        for c in range(3):
            values[c, k] = value[c]
        above = below
    return value


def substitute(ratios, values, result):
    value = [values[c, 0] for c in range(3)]
    for k in range(LEVELS):
        if k:
            value = [values[c, k] + ratios[k] * value[c] for c in range(3)]
        for c in range(3):
            result[c, pl.ds(k, TILES, stride=LEVELS), :] = value[c]


def take_matched(arrived, onehot, rank, matched):
    high, low = split(arrived[:, 0, :].T)
    slots = lax.broadcasted_iota(I32, (SLOTS, TILE), 0)
    for j in range(TILES):
        one = onehot[:, columns(j)]
        found = dot_nn(high, one) + dot_nn(low, one)
        slot = slots == rank[j : j + 1, :]
        for c in range(3):
            matched[c, j : j + 1, :] = jnp.sum(
                jnp.where(slot, found[c * SLOTS : (c + 1) * SLOTS], 0.0), axis=0, keepdims=True
            )


def send_stress(stress, onehot, rank, picked, picked_low, message):
    picked_low[3 * SLOTS :, :] = jnp.zeros((SLOTS, TILES * TILE), BF16)
    slots = lax.broadcasted_iota(I32, (SLOTS, TILE), 0)
    for j in range(TILES):
        slot = slots == rank[j : j + 1, :]
        for c in range(3):
            push = (-time_step * area_ratio) * stress[c, j : j + 1, :]
            high = push.astype(BF16).astype(F32)
            rows = slice(c * SLOTS, (c + 1) * SLOTS)
            picked[rows, columns(j)] = jnp.where(slot, high, 0.0).astype(BF16)
            picked_low[rows, columns(j)] = jnp.where(slot, push - high, 0.0).astype(BF16)
    message[:, 0, :] = dot_nt(onehot[...], picked[...]) + dot_nt(onehot[...], picked_low[...])


def kernel(
    velocity, profile_in, normal_in, height_in, pressure_in, owner_in, cell_in,
    stepped_out, wall_profile, wall_stress, requests, stresses,
    field_0, field_1, field_2, stepped, v_high, v_low,
    onehot, rank, picked, picked_low, request, gathered,
    profile, result, ratios, values, vectors, kept,
    owner, cell, height_v, normal_v, pressure_v,
    outgoing, incoming, edge_out, edge_in,
    small_sem, load_sem, profile_sem, store_sem, plane_sem, row_send, row_recv, halo_send, halo_recv,
):
    slab, span = lax.axis_index("slab"), lax.axis_index("span")
    slabs, spans = 16, 8
    me = slab * spans + span
    fields = (field_0, field_1, field_2)
    barrier = pltpu.get_barrier_semaphore()

    def others():
        for i, j in FARTHEST_FIRST:
            yield lax.rem(slab + i, slabs), lax.rem(span + j, spans)

    for to in others():
        pl.semaphore_signal(barrier, 1, device_id=to, device_id_type=MESH)

    small = [
        pltpu.make_async_copy(src, dst, small_sem.at[i])
        for i, (src, dst) in enumerate(
            ((owner_in, owner), (cell_in, cell), (height_in, height_v), (normal_in, normal_v), (pressure_in, pressure_v))
        )
    ]
    for copy in small:
        copy.start()

    loads = [
        pltpu.make_async_copy(
            velocity.at[:, :, :, columns(zb)], field_0.at[:, pl.ds(1, CX), zb, pl.ds(TOP, CY), :], load_sem.at[zb]
        )
        for zb in range(ZB)
    ]
    for copy in loads:
        copy.start()
    profile_loads = [
        pltpu.make_async_copy(
            profile_in.at[:, :, columns(j)], profile.at[:, pl.ds(j * LEVELS, LEVELS), :], profile_sem.at[j]
        )
        for j in range(TILES)
    ]
    for copy in profile_loads:
        copy.start()

    arrivals = (incoming.at[0], incoming.at[1], stresses)

    def send_row(phase, to_slab, to_span):
        pltpu.make_async_remote_copy(
            src_ref=outgoing.at[phase, to_slab * spans + to_span],
            dst_ref=arrivals[phase].at[me],
            send_sem=row_send.at[phase],
            recv_sem=row_recv.at[phase],
            device_id=(to_slab, to_span),
            device_id_type=MESH,
        ).start()

    def send_rows(phase):
        for to in others():
            send_row(phase, *to)
        if phase < 2:
            incoming[phase, me] = outgoing[phase, me]

    def await_rows(phase):
        rows = outgoing.at[phase, pl.ds(0, DEVICES - 1)]
        pltpu.make_async_copy(rows, rows, row_send.at[phase]).wait()
        rows = arrivals[phase].at[pl.ds(0, DEVICES - 1)]
        pltpu.make_async_copy(rows, rows, row_recv.at[phase]).wait()

    up_x = (lax.rem(slab + 1, slabs), span)
    down_x = (lax.rem(slab + slabs - 1, slabs), span)
    up_y = (slab, lax.rem(span + 1, spans))
    down_y = (slab, lax.rem(span + spans - 1, spans))

    def halo(n):
        field = fields[n]
        inner = pl.ds(TOP, CY)
        ends = (
            (field.at[:, CX, :, inner, :], field.at[:, 0, :, inner, :], up_x),
            (field.at[:, 1, :, inner, :], field.at[:, CX + 1, :, inner, :], down_x),
            (edge_out.at[n, 1], edge_in.at[n, 0], up_y),
            (edge_out.at[n, 0], edge_in.at[n, 1], down_y),
        )
        return [
            pltpu.make_async_remote_copy(
                src_ref=src, dst_ref=dst, send_sem=halo_send.at[n, i], recv_sem=halo_recv.at[n, i],
                device_id=to, device_id_type=MESH,
            )
            for i, (src, dst, to) in enumerate(ends)
        ]

    def send_x(copies):
        for copy in copies[:2]:
            copy.start()

    def send_y(n, copies):
        pack_rows(fields[n], edge_out.at[n])
        for copy in copies[2:]:
            copy.start()

    def await_y(n, copies):
        for copy in copies[2:]:
            copy.wait()
        unpack_rows(fields[n], edge_in.at[n], span, spans)

    def await_x(n, copies):
        for copy in copies[:2]:
            copy.wait()
        clear_planes(fields[n], slab, slabs)

    def into(field):
        def store(c, x, y, zb, value):
            field[c, x + 1, zb, pl.ds(TOP + y, 8), :] = value

        return store

    def into_result(c, x, y, zb, value):
        stepped[c, x, zb, pl.ds(y, 8), :] = value

    for copy in small[:2]:
        copy.wait()
    build_request(owner, cell, onehot, rank, picked, outgoing.at[0])
    for copy in loads:
        copy.wait()
    pl.semaphore_wait(barrier, DEVICES - 1)
    send_rows(0)
    copies = halo(0)
    send_y(0, copies)
    send_x(copies)

    for copy in small[2:] + profile_loads:
        copy.wait()
    normal, pressure, matched = vectors.at[0], vectors.at[1], vectors.at[2]
    for c in range(3):
        for j in range(TILES):
            normal[c, j : j + 1, :] = normal_v[c : c + 1, columns(j)]
            pressure[c, j : j + 1, :] = pressure_v[c : c + 1, columns(j)]
    height = height_v[...]
    inverse2 = 1.0 / (height * height)
    forcing = tangential([pressure[c] for c in range(3)], [normal[c] for c in range(3)])
    sweep_one(profile, height, inverse2, forcing, kept)
    prepare(field_0, v_high, v_low)
    await_y(0, copies)
    stage(field_0, field_0, into(field_1), None, None, INNER)

    await_rows(0)
    read_request(incoming.at[0], request)
    keep_requests = pltpu.make_async_copy(incoming.at[0], requests, store_sem.at[0])
    keep_requests.start()
    gather_cells(request, v_high, v_low, gathered, 0, EARLY, 3)
    await_x(0, copies)
    stage(field_0, field_0, into(field_1), None, None, OUTER)
    copies = halo(1)
    send_x(copies)
    send_y(1, copies)
    gather_cells(request, v_high, v_low, gathered, EARLY, SLOTS // 2, 5)
    outgoing[1, :, 0, :] = gathered[...].T
    send_rows(1)

    await_y(1, copies)
    stage(field_1, field_0, into(field_2), 0.75, 0.25, INNER)
    await_x(1, copies)
    stage(field_1, field_0, into(field_2), 0.75, 0.25, OUTER)
    copies = halo(2)
    send_x(copies)
    send_y(2, copies)

    await_rows(1)
    take_matched(incoming.at[1], onehot, rank, matched)
    target = tangential([matched[c] for c in range(3)], [normal[c] for c in range(3)])
    forcing = tangential([pressure[c] for c in range(3)], [normal[c] for c in range(3)])
    first = sweep_two(profile, height, inverse2, forcing, target, kept, ratios, values)
    scale = float(viscosity / FRAC[1]) / height
    stress = vectors.at[3]
    for c in range(3):
        stress[c] = first[c] * scale
    send_stress(stress, onehot, rank, picked, picked_low, outgoing.at[2])
    send_rows(2)
    own_row = pltpu.make_async_copy(outgoing.at[2, me], stresses.at[me], store_sem.at[1])
    own_row.start()

    for c in range(3):
        for j in range(TILES):
            wall_stress[c : c + 1, columns(j)] = stress[c, j : j + 1, :]
    def store_planes(number, begin, count):
        copies = [
            pltpu.make_async_copy(
                stepped.at[:, pl.ds(begin, count), zb],
                stepped_out.at[:, pl.ds(begin, count), :, columns(zb)],
                plane_sem.at[number, zb],
            )
            for zb in range(ZB)
        ]
        for copy in copies:
            copy.start()
        return copies

    await_y(2, copies)
    stage(field_2, field_0, into_result, 1.0 / 3.0, 2.0 / 3.0, INNER)
    stores = store_planes(0, 1, CX - 2)
    substitute(ratios, values, result)
    profile_stores = [
        pltpu.make_async_copy(
            result.at[:, pl.ds(j * LEVELS, LEVELS), :], wall_profile.at[:, :, columns(j)], profile_sem.at[j]
        )
        for j in range(TILES)
    ]
    for copy in profile_stores:
        copy.start()
    await_x(2, copies)
    stage(field_2, field_0, into_result, 1.0 / 3.0, 2.0 / 3.0, OUTER)
    stores += store_planes(1, 0, 1) + store_planes(2, CX - 1, 1)
    for copy in [keep_requests, own_row] + stores + profile_stores:
        copy.wait()
    await_rows(2)


def per_device(velocity, profile, normal, height, pressure_grad, owner_device, match_cell):
    padded = pltpu.VMEM((3, CX + 2, ZB, CY + 16, TILE), F32)
    hbm, vmem = pl.BlockSpec(memory_space=pltpu.HBM), pl.BlockSpec(memory_space=pltpu.VMEM)
    wall_shape = jax.ShapeDtypeStruct((3, LEVELS, TILES * TILE), F32)
    stress_shape = jax.ShapeDtypeStruct((3, TILES * TILE), F32)
    rows_shape = jax.ShapeDtypeStruct((DEVICES, 1, TILE), F32)
    stepped, wall_profile, wall_stress, requests, stresses = pl.pallas_call(
        kernel,
        out_shape=(jax.ShapeDtypeStruct(velocity.shape, F32), wall_shape, stress_shape, rows_shape, rows_shape),
        in_specs=[hbm] * 7,
        out_specs=(hbm, hbm, vmem, hbm, hbm),
        scratch_shapes=[
            padded, padded, padded,
            pltpu.VMEM((3, CX, ZB, CY, TILE), F32),
            pltpu.VMEM((3 * XY, NZ), BF16), pltpu.VMEM((3 * XY, NZ), BF16),
            pltpu.VMEM((DEVICES, TILES * TILE), BF16),
            pltpu.VMEM((TILES, TILE), I32),
            pltpu.VMEM((DEVICES, TILES * TILE), BF16), pltpu.VMEM((DEVICES, TILES * TILE), BF16),
            pltpu.VMEM((2 * SLOTS, TILE), I32),
            pltpu.VMEM((DEVICES, TILE), F32),
            pltpu.VMEM((3, (TILES + 1) * LEVELS, TILE), F32), pltpu.VMEM((3, (TILES + 1) * LEVELS, TILE), F32),
            pltpu.VMEM((LEVELS, TILES, TILE), F32), pltpu.VMEM((3, LEVELS, TILES, TILE), F32),
            pltpu.VMEM((4, 3, TILES, TILE), F32), pltpu.VMEM((4, TILES, TILE), F32),
            pltpu.VMEM((TILES, TILE), I32), pltpu.VMEM((TILES, TILE), I32), pltpu.VMEM((TILES, TILE), F32),
            pltpu.VMEM((3, TILES * TILE), F32), pltpu.VMEM((3, TILES * TILE), F32),
            pltpu.VMEM((3, DEVICES, 1, TILE), F32), pltpu.VMEM((3, DEVICES, 1, TILE), F32),
            pltpu.VMEM((3, 2, 3 * CX, ZB, TILE), F32), pltpu.VMEM((3, 2, 3 * CX, ZB, TILE), F32),
            pltpu.SemaphoreType.DMA((5,)), pltpu.SemaphoreType.DMA((ZB,)), pltpu.SemaphoreType.DMA((TILES,)), pltpu.SemaphoreType.DMA((2,)), pltpu.SemaphoreType.DMA((3, ZB)),
            pltpu.SemaphoreType.DMA((3,)), pltpu.SemaphoreType.DMA((3,)),
            pltpu.SemaphoreType.DMA((3, 4)), pltpu.SemaphoreType.DMA((3, 4)),
        ],
        compiler_params=pltpu.CompilerParams(
            collective_id=0, has_side_effects=True, vmem_limit_bytes=60 * MIB
        ),
    )(
        velocity,
        jnp.transpose(profile, (1, 0, 2)),
        normal,
        height.reshape(TILES, TILE),
        pressure_grad,
        owner_device.reshape(TILES, TILE),
        match_cell.reshape(TILES, TILE),
    )
    plane = pl.BlockSpec((1, CX, CY, NZ), lambda c: (c, 0, 0, 0))
    walls = pl.BlockSpec((1, LEVELS, TILES * TILE), lambda c: (c, 0, 0))
    whole = pl.BlockSpec((DEVICES, TILE), lambda c: (0, 0))
    whole_stress = pl.BlockSpec((3, TILES * TILE), lambda c: (0, 0))
    new_velocity, wall_profile, wall_stress = pl.pallas_call(
        scatter_kernel,
        grid=(3,),
        out_shape=(jax.ShapeDtypeStruct(velocity.shape, F32), wall_shape, stress_shape),
        in_specs=[whole, whole, plane, walls, whole_stress],
        out_specs=(plane, walls, whole_stress),
        scratch_shapes=[
            pltpu.VMEM((SLOTS // 2, 2 * TILE, NZ), BF16),
            pltpu.VMEM((DEVICES, TILE), F32),
            pltpu.VMEM((SLOTS, TILE), F32),
        ],
        compiler_params=pltpu.CompilerParams(vmem_limit_bytes=60 * MIB),
    )(requests.reshape(DEVICES, TILE), stresses.reshape(DEVICES, TILE), stepped, wall_profile, wall_stress)
    return new_velocity, jnp.transpose(wall_profile, (1, 0, 2)), wall_stress


def solution(mesh):
    return jax.shard_map(
        per_device,
        mesh=mesh,
        in_specs=(
            P(None, "slab", "span", None),
            P(None, None, ("slab", "span")),
            P(None, ("slab", "span")),
            P(("slab", "span")),
            P(None, ("slab", "span")),
            P(("slab", "span"), None),
            P(("slab", "span")),
        ),
        out_specs=(
            P(None, "slab", "span", None),
            P(None, None, ("slab", "span")),
            P(None, ("slab", "span")),
        ),
        check_vma=False,
    )
```

```python
import jax
import jax.numpy as jnp
import numpy as np
from jax import lax
from jax.experimental import pallas as pl
from jax.experimental.pallas import tpu as pltpu
from jax.sharding import PartitionSpec as P

MESH = pl.DeviceIdType.MESH
BF16, F32, I32 = jnp.bfloat16, jnp.float32, jnp.int32

DEVICES = 128
SLOTS = 32
TILE = 128
TILES = 16
LEVELS = 32
CX, CY, ZB = 8, 32, 4
XY = CX * CY
NZ = 512
TOP = 8
MIB = 1 << 20
INNER, OUTER = range(1, CX - 1), range(0, CX, CX - 1)
EARLY = 6

time_step = 0.1
viscosity = 0.001
smag_coef = 0.02
kappa_coef = 0.41
damping_plus = 26.0
stretch = 1.12
area_ratio = 4.0

FRAC = (stretch ** np.arange(LEVELS + 2) - 1.0) / (stretch ** (LEVELS + 1) - 1.0)
SPACING = FRAC[1:] - FRAC[:-1]
FACE = 0.5 * (FRAC[1:] + FRAC[:-1])
SPAN = 0.5 * (FRAC[2:] - FRAC[:-2])
LOWER = [float(v) for v in time_step / (SPACING[:-1] * SPAN)]
UPPER = [float(v) for v in time_step / (SPACING[1:] * SPAN)]


def dot_nn(a, b):
    return lax.dot_general(a, b, (((1,), (0,)), ((), ())), preferred_element_type=F32)


def dot_nt(a, b):
    return lax.dot_general(a, b, (((1,), (1,)), ((), ())), preferred_element_type=F32)


def split(value):
    high = value.astype(BF16)
    return high, (value - high.astype(F32)).astype(BF16)


def hops(offset):
    slab, span = offset
    return sum(min(step, 4 - step) for step in (slab // 4, slab % 4, span // 2)) + span % 2 / 2


FARTHEST_FIRST = sorted(((i, j) for i in range(16) for j in range(8) if i or j), key=hops, reverse=True)


def columns(j):
    return pl.ds(j * TILE, TILE)


def build_request(owner, cell, onehot, rank, picked, message):
    rows = lax.broadcasted_iota(I32, (TILE, TILE), 0)
    lanes = lax.broadcasted_iota(I32, (TILE, TILE), 1)
    earlier = jnp.where(rows < lanes, 1.0, 0.0).astype(BF16)
    summing = jnp.concatenate([earlier, jnp.ones((TILE, TILE), BF16)], axis=1)
    slots = lax.broadcasted_iota(I32, (SLOTS, TILE), 0)
    picked[3 * SLOTS :, :] = jnp.zeros((SLOTS, TILES * TILE), BF16)
    taken = jnp.zeros((TILE, TILE), F32)
    for j in range(TILES):
        mine = rows == owner[j : j + 1, :]
        one = jnp.where(mine, 1.0, 0.0).astype(BF16)
        onehot[:, columns(j)] = one
        counts = dot_nn(one, summing)
        place = jnp.sum(jnp.where(mine, counts[:, :TILE] + taken, 0.0), axis=0, keepdims=True).astype(I32)
        taken = taken + counts[:, TILE:]
        rank[j : j + 1, :] = place
        at = cell[j : j + 1, :]
        slot = slots == place
        depth = at & (NZ - 1)
        for part, value in enumerate((at >> 9, depth & (NZ - 2), depth & 1)):
            picked[part * SLOTS : (part + 1) * SLOTS, columns(j)] = jnp.where(slot, value.astype(F32), 0.0).astype(BF16)
    message[:, 0, :] = dot_nt(onehot[...], picked[...])


def read_request(arrived, request):
    turned = arrived[:, 0, :].T
    request[0:SLOTS, :] = turned[0:SLOTS].astype(I32)
    request[SLOTS : 2 * SLOTS, :] = (turned[SLOTS : 2 * SLOTS] + turned[2 * SLOTS : 3 * SLOTS]).astype(I32)


def gather_cells(request, v_high, v_low, gathered, begin, end, step):
    depths = lax.broadcasted_iota(I32, (NZ, TILE), 0)
    planes = lax.broadcasted_iota(I32, (XY, TILE), 0)

    @pl.loop(begin, end, step=step)
    def _(first):
        for i in range(step):
            pair = first + i
            slots = (2 * pair, 2 * pair + 1)
            hots = [
                jnp.where(depths == request[pl.ds(SLOTS + slot, 1), :], 1.0, 0.0).astype(BF16) for slot in slots
            ]
            hot = jnp.concatenate(hots, axis=1)
            for c in range(3):
                part = slice(c * XY, (c + 1) * XY)
                found = dot_nn(v_high[part, :], hot) + dot_nn(v_low[part, :], hot)
                for half, slot in enumerate(slots):
                    where = planes == request[pl.ds(slot, 1), :]
                    gathered[pl.ds(c * SLOTS + slot, 1), :] = jnp.sum(
                        jnp.where(where, found[:, half * TILE : (half + 1) * TILE], 0.0), axis=0, keepdims=True
                    )


def scatter_kernel(requests, stresses, base, wall_in, stress_in, out, wall_out, stress_out, depth_hot, pushes, planes_of):
    c = pl.program_id(0)
    wall_out[...] = wall_in[...]

    @pl.when(c == 0)
    def _():
        stress_out[...] = stress_in[...]
        pushes[...] = stresses[...].T
        planes_of[...] = requests[...].T[0:SLOTS]
        depths = lax.broadcasted_iota(I32, (TILE, 256), 1).astype(F32).astype(BF16)
        depth = requests[:, SLOTS : 2 * SLOTS] + requests[:, 2 * SLOTS : 3 * SLOTS]
        for slot in range(SLOTS):
            for side in range(2):
                here = depth[:, slot : slot + 1] - 256.0 * side
                here = jnp.where((here >= 0.0) & (here < 256.0), here, -1.0)
                here = jnp.broadcast_to(here, (TILE, 256)).astype(BF16)
                hot = jnp.where(depths == here, jnp.ones((), BF16), jnp.zeros((), BF16))
                depth_hot[slot // 2, columns(slot % 2), side * 256 : (side + 1) * 256] = hot

    planes = lax.broadcasted_iota(I32, (XY, TILE), 0).astype(F32).astype(BF16)
    zero = jnp.zeros((), BF16)
    total = jnp.zeros((XY, NZ), F32)
    for pair in range(SLOTS // 2):
        highs, lows = [], []
        for slot in (2 * pair, 2 * pair + 1):
            high, low = split(pushes[pl.ds(c * SLOTS + slot, 1), :])
            where = planes == planes_of[slot : slot + 1, :].astype(BF16)
            highs.append(jnp.where(where, high, zero))
            lows.append(jnp.where(where, low, zero))
        for part in (highs, lows):
            total = total + dot_nn(jnp.concatenate(part, axis=1), depth_hot[pair])
    for x in range(CX):
        out[0, x] = base[0, x] + total[x * CY : (x + 1) * CY]


def prepare(field, v_high, v_low):
    @pl.loop(0, 3 * CX)
    def _(i):
        c, x = i // CX, i % CX
        for zb in range(ZB):
            high, low = split(field[c, x + 1, zb, TOP : TOP + CY, :])
            rows = pl.ds(pl.multiple_of(i * CY, CY), CY)
            v_high[rows, columns(zb)] = high
            v_low[rows, columns(zb)] = low


def pack_rows(field, edge):
    for side, row in ((0, TOP), (1, TOP + CY - 1)):
        for c in range(3):
            for x in range(CX):
                edge[side, c * CX + x] = field[c, x + 1, :, row, :]


def unpack_rows(field, edge, span, spans):
    for side, row in ((0, TOP - 1), (1, TOP + CY)):
        for c in range(3):
            for x in range(CX):
                field[c, x + 1, :, row, :] = edge[side, c * CX + x]
    zero_row = jnp.zeros((CX, ZB, TILE), F32)
    for at, row in ((0, TOP - 1), (spans - 1, TOP + CY)):

        @pl.when(span == at)
        def _():
            for c in range(3):
                field[c, 1 : CX + 1, :, row, :] = zero_row


def clear_planes(field, slab, slabs):
    zero_plane = jnp.zeros((ZB, CY, TILE), F32)
    for at, plane in ((0, 0), (slabs - 1, CX + 1)):

        @pl.when(slab == at)
        def _():
            for c in range(3):
                field[c, plane, :, TOP : TOP + CY, :] = zero_plane


def stage(field, first, store, keep, mix, planes):
    lane = lax.broadcasted_iota(I32, (8, TILE), 1)
    at_start, at_end = lane == 0, lane == TILE - 1
    zeros = jnp.zeros((8, TILE), F32)

    @pl.loop(0, len(planes))
    def _(i):
        x = planes.start + i * planes.step
        for y in range(0, CY, 8):
            here = pl.ds(TOP + y, 8)
            center = [[field[c, x + 1, zb, here, :] for zb in range(ZB)] for c in range(3)]
            ahead = [[pltpu.roll(v, TILE - 1, 1) for v in row] for row in center]
            behind = [[pltpu.roll(v, 1, 1) for v in row] for row in center]
            for zb in range(ZB):
                mid = [center[c][zb] for c in range(3)]
                shear = zeros
                lap, grads = [], []
                for c in range(3):
                    xp, xm = field[c, x + 2, zb, here, :], field[c, x, zb, here, :]
                    yp, ym = field[c, x + 1, zb, pl.ds(TOP + y + 1, 8), :], field[c, x + 1, zb, pl.ds(TOP + y - 1, 8), :]
                    zp = jnp.where(at_end, ahead[c][zb + 1] if zb + 1 < ZB else zeros, ahead[c][zb])
                    zm = jnp.where(at_start, behind[c][zb - 1] if zb else zeros, behind[c][zb])
                    gx, gy, gz = xp - xm, yp - ym, zp - zm
                    shear = shear + (gx * gx + gy * gy + gz * gz)
                    lap.append(((xp + xm) + (yp + ym)) + ((zp + zm) - 6.0 * mid[c]))
                    grads.append(mid[0] * gx + mid[1] * gy + mid[2] * gz)
                eddy = viscosity + (0.5 * smag_coef) * jnp.sqrt(shear)
                for c in range(3):
                    moved = mid[c] + time_step * (eddy * lap[c] - 0.5 * grads[c])
                    if keep:
                        moved = keep * first[c, x + 1, zb, here, :] + mix * moved
                    store(c, x, y, zb, moved)


def tangential(vector, normal):
    along = vector[0] * normal[0] + vector[1] * normal[1] + vector[2] * normal[2]
    return [vector[c] - along * normal[c] for c in range(3)]


def level(ref, c, k):
    return ref[c, pl.ds(k, TILES, stride=LEVELS), :]


def diffusivity(first, height, inverse2):
    ratio = float((viscosity / FRAC[1]) ** 2)
    square = (first[0] * first[0] + first[1] * first[1] + first[2] * first[2]) * inverse2 * ratio
    scaled = height * jnp.sqrt(jnp.sqrt(square))

    def at(k):
        damping = 1.0 - jnp.exp(scaled * float(-FACE[k] / (viscosity * damping_plus)))
        return viscosity + (float(kappa_coef * FACE[k]) * scaled) * (damping * damping)

    return at


def reciprocal(value):
    guess = pl.reciprocal(value, approx=True)
    return guess * (2.0 - value * guess)


def sweep_one(profile, height, inverse2, forcing, kept):
    at = diffusivity([level(profile, c, 0) for c in range(3)], height, inverse2)
    above = at(LEVELS)
    ratio = jnp.zeros((TILES, TILE), F32)
    value = [jnp.zeros((TILES, TILE), F32)] * 3
    answer = jnp.ones((TILES, TILE), F32)
    for k in range(LEVELS - 1, -1, -1):
        below = at(k)
        low = (below * inverse2) * LOWER[k]
        up = (above * inverse2) * UPPER[k]
        inverse = reciprocal(1.0 + low + up * (1.0 - ratio))
        ratio = low * inverse
        value = [(level(profile, c, k) - time_step * forcing[c] + up * value[c]) * inverse for c in range(3)]
        answer = answer * (up * inverse)
        above = below
    for c in range(3):
        kept[c] = value[c]
    kept[3] = answer


def sweep_two(profile, height, inverse2, forcing, target, kept, ratios, values):
    at = diffusivity([kept[c] + kept[3] * target[c] for c in range(3)], height, inverse2)
    above = at(LEVELS)
    ratio = jnp.zeros((TILES, TILE), F32)
    value = target
    for k in range(LEVELS - 1, -1, -1):
        below = at(k)
        low = (below * inverse2) * LOWER[k]
        up = (above * inverse2) * UPPER[k]
        inverse = reciprocal(1.0 + low + up * (1.0 - ratio))
        ratio = low * inverse
        ratios[k] = ratio
        value = [(level(profile, c, k) - time_step * forcing[c] + up * value[c]) * inverse for c in range(3)]
        for c in range(3):
            values[c, k] = value[c]
        above = below
    return value


def substitute(ratios, values, result):
    value = [values[c, 0] for c in range(3)]
    for k in range(LEVELS):
        if k:
            value = [values[c, k] + ratios[k] * value[c] for c in range(3)]
        for c in range(3):
            result[c, pl.ds(k, TILES, stride=LEVELS), :] = value[c]


def take_matched(arrived, onehot, rank, matched):
    high, low = split(arrived[:, 0, :].T)
    slots = lax.broadcasted_iota(I32, (SLOTS, TILE), 0)
    for j in range(TILES):
        one = onehot[:, columns(j)]
        found = dot_nn(high, one) + dot_nn(low, one)
        slot = slots == rank[j : j + 1, :]
        for c in range(3):
            matched[c, j : j + 1, :] = jnp.sum(
                jnp.where(slot, found[c * SLOTS : (c + 1) * SLOTS], 0.0), axis=0, keepdims=True
            )


def send_stress(stress, onehot, rank, picked, picked_low, message):
    picked_low[3 * SLOTS :, :] = jnp.zeros((SLOTS, TILES * TILE), BF16)
    slots = lax.broadcasted_iota(I32, (SLOTS, TILE), 0)
    for j in range(TILES):
        slot = slots == rank[j : j + 1, :]
        for c in range(3):
            push = (-time_step * area_ratio) * stress[c, j : j + 1, :]
            high = push.astype(BF16).astype(F32)
            rows = slice(c * SLOTS, (c + 1) * SLOTS)
            picked[rows, columns(j)] = jnp.where(slot, high, 0.0).astype(BF16)
            picked_low[rows, columns(j)] = jnp.where(slot, push - high, 0.0).astype(BF16)
    message[:, 0, :] = dot_nt(onehot[...], picked[...]) + dot_nt(onehot[...], picked_low[...])


def kernel(
    velocity, profile_in, normal_in, height_in, pressure_in, owner_in, cell_in,
    stepped_out, wall_profile, wall_stress, requests, stresses,
    field_0, field_1, field_2, stepped, v_high, v_low,
    onehot, rank, picked, picked_low, request, gathered,
    profile, result, ratios, values, vectors, kept,
    owner, cell, height_v, normal_v, pressure_v,
    outgoing, incoming, edge_out, edge_in,
    small_sem, load_sem, profile_sem, store_sem, plane_sem, row_send, row_recv, halo_send, halo_recv,
):
    slab, span = lax.axis_index("slab"), lax.axis_index("span")
    slabs, spans = 16, 8
    me = slab * spans + span
    fields = (field_0, field_1, field_2)
    barrier = pltpu.get_barrier_semaphore()

    def others():
        for i, j in FARTHEST_FIRST:
            yield lax.rem(slab + i, slabs), lax.rem(span + j, spans)

    for to in others():
        pl.semaphore_signal(barrier, 1, device_id=to, device_id_type=MESH)

    small = [
        pltpu.make_async_copy(src, dst, small_sem.at[i])
        for i, (src, dst) in enumerate(
            ((owner_in, owner), (cell_in, cell), (height_in, height_v), (normal_in, normal_v), (pressure_in, pressure_v))
        )
    ]
    for copy in small:
        copy.start()

    loads = [
        pltpu.make_async_copy(
            velocity.at[:, :, :, columns(zb)], field_0.at[:, pl.ds(1, CX), zb, pl.ds(TOP, CY), :], load_sem.at[zb]
        )
        for zb in range(ZB)
    ]
    for copy in loads:
        copy.start()
    profile_loads = [
        pltpu.make_async_copy(
            profile_in.at[:, :, columns(j)], profile.at[:, pl.ds(j * LEVELS, LEVELS), :], profile_sem.at[j]
        )
        for j in range(TILES)
    ]
    for copy in profile_loads:
        copy.start()

    arrivals = (incoming.at[0], incoming.at[1], stresses)

    def send_row(phase, to_slab, to_span):
        pltpu.make_async_remote_copy(
            src_ref=outgoing.at[phase, to_slab * spans + to_span],
            dst_ref=arrivals[phase].at[me],
            send_sem=row_send.at[phase],
            recv_sem=row_recv.at[phase],
            device_id=(to_slab, to_span),
            device_id_type=MESH,
        ).start()

    def send_rows(phase):
        for to in others():
            send_row(phase, *to)
        if phase < 2:
            incoming[phase, me] = outgoing[phase, me]

    def await_rows(phase):
        rows = outgoing.at[phase, pl.ds(0, DEVICES - 1)]
        pltpu.make_async_copy(rows, rows, row_send.at[phase]).wait()
        rows = arrivals[phase].at[pl.ds(0, DEVICES - 1)]
        pltpu.make_async_copy(rows, rows, row_recv.at[phase]).wait()

    up_x = (lax.rem(slab + 1, slabs), span)
    down_x = (lax.rem(slab + slabs - 1, slabs), span)
    up_y = (slab, lax.rem(span + 1, spans))
    down_y = (slab, lax.rem(span + spans - 1, spans))

    def halo(n):
        field = fields[n]
        inner = pl.ds(TOP, CY)
        ends = (
            (field.at[:, CX, :, inner, :], field.at[:, 0, :, inner, :], up_x),
            (field.at[:, 1, :, inner, :], field.at[:, CX + 1, :, inner, :], down_x),
            (edge_out.at[n, 1], edge_in.at[n, 0], up_y),
            (edge_out.at[n, 0], edge_in.at[n, 1], down_y),
        )
        return [
            pltpu.make_async_remote_copy(
                src_ref=src, dst_ref=dst, send_sem=halo_send.at[n, i], recv_sem=halo_recv.at[n, i],
                device_id=to, device_id_type=MESH,
            )
            for i, (src, dst, to) in enumerate(ends)
        ]

    def send_x(copies):
        for copy in copies[:2]:
            copy.start()

    def send_y(n, copies):
        pack_rows(fields[n], edge_out.at[n])
        for copy in copies[2:]:
            copy.start()

    def await_y(n, copies):
        for copy in copies[2:]:
            copy.wait()
        unpack_rows(fields[n], edge_in.at[n], span, spans)

    def await_x(n, copies):
        for copy in copies[:2]:
            copy.wait()
        clear_planes(fields[n], slab, slabs)

    def into(field):
        def store(c, x, y, zb, value):
            field[c, x + 1, zb, pl.ds(TOP + y, 8), :] = value

        return store

    def into_result(c, x, y, zb, value):
        stepped[c, x, zb, pl.ds(y, 8), :] = value

    for copy in small[:2]:
        copy.wait()
    build_request(owner, cell, onehot, rank, picked, outgoing.at[0])
    for copy in loads:
        copy.wait()
    pl.semaphore_wait(barrier, DEVICES - 1)
    send_rows(0)
    copies = halo(0)
    send_y(0, copies)
    send_x(copies)

    for copy in small[2:] + profile_loads:
        copy.wait()
    normal, pressure, matched = vectors.at[0], vectors.at[1], vectors.at[2]
    for c in range(3):
        for j in range(TILES):
            normal[c, j : j + 1, :] = normal_v[c : c + 1, columns(j)]
            pressure[c, j : j + 1, :] = pressure_v[c : c + 1, columns(j)]
    height = height_v[...]
    inverse2 = 1.0 / (height * height)
    forcing = tangential([pressure[c] for c in range(3)], [normal[c] for c in range(3)])
    sweep_one(profile, height, inverse2, forcing, kept)
    prepare(field_0, v_high, v_low)
    await_y(0, copies)
    stage(field_0, field_0, into(field_1), None, None, INNER)

    await_rows(0)
    read_request(incoming.at[0], request)
    keep_requests = pltpu.make_async_copy(incoming.at[0], requests, store_sem.at[0])
    keep_requests.start()
    gather_cells(request, v_high, v_low, gathered, 0, EARLY, 3)
    await_x(0, copies)
    stage(field_0, field_0, into(field_1), None, None, OUTER)
    copies = halo(1)
    send_x(copies)
    send_y(1, copies)
    gather_cells(request, v_high, v_low, gathered, EARLY, SLOTS // 2, 5)
    outgoing[1, :, 0, :] = gathered[...].T
    send_rows(1)

    await_y(1, copies)
    stage(field_1, field_0, into(field_2), 0.75, 0.25, INNER)
    await_x(1, copies)
    stage(field_1, field_0, into(field_2), 0.75, 0.25, OUTER)
    copies = halo(2)
    send_x(copies)
    send_y(2, copies)

    await_rows(1)
    take_matched(incoming.at[1], onehot, rank, matched)
    target = tangential([matched[c] for c in range(3)], [normal[c] for c in range(3)])
    forcing = tangential([pressure[c] for c in range(3)], [normal[c] for c in range(3)])
    first = sweep_two(profile, height, inverse2, forcing, target, kept, ratios, values)
    scale = float(viscosity / FRAC[1]) / height
    stress = vectors.at[3]
    for c in range(3):
        stress[c] = first[c] * scale
    send_stress(stress, onehot, rank, picked, picked_low, outgoing.at[2])
    send_rows(2)
    own_row = pltpu.make_async_copy(outgoing.at[2, me], stresses.at[me], store_sem.at[1])
    own_row.start()

    for c in range(3):
        for j in range(TILES):
            wall_stress[c : c + 1, columns(j)] = stress[c, j : j + 1, :]
    def store_planes(number, begin, count):
        copies = [
            pltpu.make_async_copy(
                stepped.at[:, pl.ds(begin, count), zb],
                stepped_out.at[:, pl.ds(begin, count), :, columns(zb)],
                plane_sem.at[number, zb],
            )
            for zb in range(ZB)
        ]
        for copy in copies:
            copy.start()
        return copies

    await_y(2, copies)
    stage(field_2, field_0, into_result, 1.0 / 3.0, 2.0 / 3.0, INNER)
    stores = store_planes(0, 1, CX - 2)
    substitute(ratios, values, result)
    profile_stores = [
        pltpu.make_async_copy(
            result.at[:, pl.ds(j * LEVELS, LEVELS), :], wall_profile.at[:, :, columns(j)], profile_sem.at[j]
        )
        for j in range(TILES)
    ]
    for copy in profile_stores:
        copy.start()
    await_x(2, copies)
    stage(field_2, field_0, into_result, 1.0 / 3.0, 2.0 / 3.0, OUTER)
    stores += store_planes(1, 0, 1) + store_planes(2, CX - 1, 1)
    for copy in [keep_requests, own_row] + stores + profile_stores:
        copy.wait()
    await_rows(2)


def per_device(velocity, profile, normal, height, pressure_grad, owner_device, match_cell):
    padded = pltpu.VMEM((3, CX + 2, ZB, CY + 16, TILE), F32)
    hbm, vmem = pl.BlockSpec(memory_space=pltpu.HBM), pl.BlockSpec(memory_space=pltpu.VMEM)
    wall_shape = jax.ShapeDtypeStruct((3, LEVELS, TILES * TILE), F32)
    stress_shape = jax.ShapeDtypeStruct((3, TILES * TILE), F32)
    rows_shape = jax.ShapeDtypeStruct((DEVICES, 1, TILE), F32)
    stepped, wall_profile, wall_stress, requests, stresses = pl.pallas_call(
        kernel,
        out_shape=(jax.ShapeDtypeStruct(velocity.shape, F32), wall_shape, stress_shape, rows_shape, rows_shape),
        in_specs=[hbm] * 7,
        out_specs=(hbm, hbm, vmem, hbm, hbm),
        scratch_shapes=[
            padded, padded, padded,
            pltpu.VMEM((3, CX, ZB, CY, TILE), F32),
            pltpu.VMEM((3 * XY, NZ), BF16), pltpu.VMEM((3 * XY, NZ), BF16),
            pltpu.VMEM((DEVICES, TILES * TILE), BF16),
            pltpu.VMEM((TILES, TILE), I32),
            pltpu.VMEM((DEVICES, TILES * TILE), BF16), pltpu.VMEM((DEVICES, TILES * TILE), BF16),
            pltpu.VMEM((2 * SLOTS, TILE), I32),
            pltpu.VMEM((DEVICES, TILE), F32),
            pltpu.VMEM((3, (TILES + 1) * LEVELS, TILE), F32), pltpu.VMEM((3, (TILES + 1) * LEVELS, TILE), F32),
            pltpu.VMEM((LEVELS, TILES, TILE), F32), pltpu.VMEM((3, LEVELS, TILES, TILE), F32),
            pltpu.VMEM((4, 3, TILES, TILE), F32), pltpu.VMEM((4, TILES, TILE), F32),
            pltpu.VMEM((TILES, TILE), I32), pltpu.VMEM((TILES, TILE), I32), pltpu.VMEM((TILES, TILE), F32),
            pltpu.VMEM((3, TILES * TILE), F32), pltpu.VMEM((3, TILES * TILE), F32),
            pltpu.VMEM((3, DEVICES, 1, TILE), F32), pltpu.VMEM((3, DEVICES, 1, TILE), F32),
            pltpu.VMEM((3, 2, 3 * CX, ZB, TILE), F32), pltpu.VMEM((3, 2, 3 * CX, ZB, TILE), F32),
            pltpu.SemaphoreType.DMA((5,)), pltpu.SemaphoreType.DMA((ZB,)), pltpu.SemaphoreType.DMA((TILES,)), pltpu.SemaphoreType.DMA((2,)), pltpu.SemaphoreType.DMA((3, ZB)),
            pltpu.SemaphoreType.DMA((3,)), pltpu.SemaphoreType.DMA((3,)),
            pltpu.SemaphoreType.DMA((3, 4)), pltpu.SemaphoreType.DMA((3, 4)),
        ],
        compiler_params=pltpu.CompilerParams(
            collective_id=0, has_side_effects=True, vmem_limit_bytes=60 * MIB
        ),
    )(
        velocity,
        jnp.transpose(profile, (1, 0, 2)),
        normal,
        height.reshape(TILES, TILE),
        pressure_grad,
        owner_device.reshape(TILES, TILE),
        match_cell.reshape(TILES, TILE),
    )
    plane = pl.BlockSpec((1, CX, CY, NZ), lambda c: (c, 0, 0, 0))
    walls = pl.BlockSpec((1, LEVELS, TILES * TILE), lambda c: (c, 0, 0))
    whole = pl.BlockSpec((DEVICES, TILE), lambda c: (0, 0))
    whole_stress = pl.BlockSpec((3, TILES * TILE), lambda c: (0, 0))
    new_velocity, wall_profile, wall_stress = pl.pallas_call(
        scatter_kernel,
        grid=(3,),
        out_shape=(jax.ShapeDtypeStruct(velocity.shape, F32), wall_shape, stress_shape),
        in_specs=[whole, whole, plane, walls, whole_stress],
        out_specs=(plane, walls, whole_stress),
        scratch_shapes=[
            pltpu.VMEM((SLOTS // 2, 2 * TILE, NZ), BF16),
            pltpu.VMEM((DEVICES, TILE), F32),
            pltpu.VMEM((SLOTS, TILE), F32),
        ],
        compiler_params=pltpu.CompilerParams(vmem_limit_bytes=60 * MIB),
    )(requests.reshape(DEVICES, TILE), stresses.reshape(DEVICES, TILE), stepped, wall_profile, wall_stress)
    return new_velocity, jnp.transpose(wall_profile, (1, 0, 2)), wall_stress


def solution(mesh):
    return jax.shard_map(
        per_device,
        mesh=mesh,
        in_specs=(
            P(None, "slab", "span", None),
            P(None, None, ("slab", "span")),
            P(None, ("slab", "span")),
            P(("slab", "span")),
            P(None, ("slab", "span")),
            P(("slab", "span"), None),
            P(("slab", "span")),
        ),
        out_specs=(
            P(None, "slab", "span", None),
            P(None, None, ("slab", "span")),
            P(None, ("slab", "span")),
        ),
        check_vma=False,
    )
```
